512 devices in a mesh: chan: 64 (over y_hi, z, core), tm: 8 (over y_lo, x).
Axes of the slice: x: 4, y: 8 (y_hi: 4, y_lo: 2; y = y_hi * 2 + y_lo), z: 8, core: 2. Of those that a mesh axis runs over, the one named last changes fastest.
Arguments:
- samples: bfloat16 [1024, 16384], P('chan', 'tm'), may hold values from -6 to 6
- fir_taps: float32 [96], replicated, may hold values from -0.625 to 0.625
- plan: int32 [4], replicated, may hold values from 1 to 63, as said below
Outputs:
- self_corr: float32 [1024, 16, 129], P(('chan', 'tm'))
- pair_corr: float32 [4, 1024, 16, 129], P(None, ('chan', 'tm'))
The draws below stay inside these ranges and needn't reach their ends.
Inputs may be any that keep to these rules, and one draw needn't show every extreme that they name: Round r pairs block g with block g XOR plan[r]; the masks of the rounds are distinct, and the values 1 and 63 both occur.
All inputs are finite; a program needn't handle non-finite values.
Results may differ from the reference program's by a relative error of at most 0.0043.
Values may be sent and summed in bfloat16 or wider, within the bound.
A program may use at most 128 MiB of HBM per device.

```python
import math
import jax
import jax.numpy as jnp
from jax import lax

CH_DEV = 16
SEG = 1024
TAPS = 96
LAGS = 129
ROUNDS = 4
HALF = 513
CHANNELS = 1024
SEGMENTS = 16
TIME = 16384
N_CHAN = 64


def draw_plan(key, part):
    key = jax.random.fold_in(key, 11)
    key_masks, key_order = jax.random.split(key)
    inner_masks = jax.random.permutation(key_masks, N_CHAN - 3)[:ROUNDS - 2] + 2
    all_masks = jnp.concatenate([jnp.array([1, N_CHAN - 1], jnp.int32), inner_masks.astype(jnp.int32)])
    return jax.random.permutation(key_order, all_masks).astype(jnp.int32)


def block_scale(stream_key, shape, pieces, low, top_value):
    factor_of = 1.0
    for axis_at, parts in pieces:
        draws = jax.random.uniform(jax.random.fold_in(jax.random.fold_in(stream_key, 6), axis_at), (parts,), jnp.float32, low / len(pieces), top_value / len(pieces))
        factor_of = factor_of * jnp.repeat(jnp.exp(draws), shape[axis_at] // parts).reshape((-1,) + (1,) * (len(shape) - 1 - axis_at))
    return factor_of


def bell_draw(stream_key, dims, spread, bound, cuts=(), held_as=jnp.bfloat16):
    loudness = block_scale(stream_key, dims, cuts, -0.22, 0.18) if cuts else 1.0
    result = jax.random.normal(stream_key, dims, jnp.float32) * spread * loudness
    return jnp.minimum(jnp.maximum(result, -bound), bound).astype(held_as)


def setup_inputs(seed: int = 0) -> dict:
    key_of = jax.random.split(jax.random.key(seed), 4)
    samples = bell_draw(key_of[0], (CHANNELS, TIME), 1.0, 6.0, ((0, 64), (1, 8)))
    fir_taps = bell_draw(key_of[1], (TAPS,), TAPS ** -0.5, 0.625, (), jnp.float32)
    plan = draw_plan(jax.random.fold_in(key_of[3], 71), 0)
    return {"samples": samples, "fir_taps": fir_taps, "plan": plan}


def dft_matrix(length, half):
    sample_index = jnp.arange(length, dtype=jnp.int32)[:, None]
    freq_index = jnp.arange(half, dtype=jnp.int32)[None, :]
    angles = 2.0 * math.pi / length * (sample_index * freq_index % length).astype(jnp.float32)
    return jnp.concatenate([jnp.cos(angles), -jnp.sin(angles)], axis=1)

def fir_filter(extended, fir_taps, length):
    rim_width = fir_taps.shape[0] - 1
    widened = extended.astype(jnp.float32)
    summed = jnp.zeros((extended.shape[0], length), jnp.float32)
    for tap_index in range(rim_width + 1):
        begin = rim_width - tap_index
        summed = summed + fir_taps[tap_index] * widened[:, begin:begin + length]
    return summed

def whiten(filtered, matrix):
    spectrum = jnp.dot(filtered, matrix, precision=lax.Precision.HIGHEST, preferred_element_type=jnp.float32)
    half = matrix.shape[1] // 2
    real_part = spectrum[:, :half]
    imag_part = spectrum[:, half:]
    energy = real_part * real_part + imag_part * imag_part
    water_level = 0.1 * lax.optimization_barrier(jnp.mean(energy, axis=1, keepdims=True))
    inverse_amp = lax.rsqrt(energy + water_level + 1e-06)
    return jnp.concatenate([real_part * inverse_amp, imag_part * inverse_amp], axis=1).astype(jnp.bfloat16)

def rotate(spectra, lag_count):
    half = spectra.shape[-1] // 2
    length = 2 * (half - 1)
    lag_value = jnp.arange(lag_count, dtype=jnp.int32) - lag_count // 2
    freq_index = jnp.arange(half, dtype=jnp.int32)
    angles = 2.0 * math.pi / length * (lag_value[:, None] * freq_index[None, :] % length).astype(jnp.float32)
    edges = (freq_index == 0) | (freq_index == half - 1)
    weight = jnp.where(edges, 1.0, 2.0).astype(jnp.float32) / length
    cosine = jnp.cos(angles) * weight
    sinus = jnp.sin(angles) * weight
    real_part = spectra[..., :half].astype(jnp.float32)[..., None, :]
    imag_part = spectra[..., half:].astype(jnp.float32)[..., None, :]
    rot_real = real_part * cosine - imag_part * sinus
    rot_imag = imag_part * cosine + real_part * sinus
    return jnp.concatenate([rot_real, rot_imag], axis=-1).astype(jnp.bfloat16)

def correlate_stack(rotated, partner):
    return jnp.einsum('talk,tbk->abl', rotated.astype(jnp.float32), partner.astype(jnp.float32), precision=lax.Precision.HIGHEST)

def reference(samples, fir_taps, plan):
    leading = jnp.zeros((CHANNELS, TAPS - 1), jnp.bfloat16)
    filtered = fir_filter(jnp.concatenate([leading, samples], axis=1), fir_taps, TIME)
    segments = filtered.reshape(CHANNELS, SEGMENTS, SEG).transpose(1, 0, 2).reshape(SEGMENTS * CHANNELS, SEG)
    spectra = whiten(segments, dft_matrix(SEG, HALF))
    spectra = spectra.reshape(SEGMENTS, N_CHAN, CH_DEV, 2 * HALF).transpose(1, 0, 2, 3)

    def per_block(block_index):
        own_spectra = spectra[block_index]
        rotated = rotate(own_spectra, LAGS)
        self_term = correlate_stack(rotated, own_spectra)
        pair_terms = []
        for round_index in range(ROUNDS):
            partner_index = jnp.bitwise_xor(block_index, plan[round_index]).astype(jnp.int32)
            pair_terms.append(correlate_stack(rotated, spectra[partner_index]))
        return (self_term, jnp.stack(pair_terms))
    self_all, pair_all = lax.map(per_block, jnp.arange(N_CHAN, dtype=jnp.int32))
    self_corr = self_all.reshape(CHANNELS, CH_DEV, LAGS)
    pair_corr = pair_all.transpose(1, 0, 2, 3, 4).reshape(ROUNDS, CHANNELS, CH_DEV, LAGS)
    return (self_corr, pair_corr)
```

```python
import functools

import jax
import jax.numpy as jnp
import ml_dtypes
import numpy as np
from jax import lax
from jax.experimental import pallas as pl
from jax.experimental.pallas import tpu as pltpu
from jax.sharding import PartitionSpec as P

MESH = pl.DeviceIdType.MESH
BF16 = jnp.bfloat16
F32 = jnp.float32

CH = 16
SEG = 1024
LAGS = 129
ROUNDS = 4
TM = 8
LANES = 128
TILES = 16
GROUPS = 4
HOP_CORE, HOP_Z1, HOP_Z2, HOP_Z6, HOP_Z7, HOP_Y1, HOP_Y3 = 1, 2, 4, 12, 14, 16, 48
CHAN_HOPS = (HOP_CORE, HOP_Z1, HOP_Z2, HOP_Z6, HOP_Z7, HOP_Y1, HOP_Y3)
STAGES = (
    (("A", HOP_Z1), ("B", HOP_Y1), ("F", HOP_Z7)),
    (("A", HOP_Z2), ("B", HOP_Y3)),
    (("A", HOP_Z6), ("B", HOP_Z1), ("F", HOP_Y3)),
    (("A", HOP_Y1), ("B", HOP_Z2)),
    (("A", HOP_Y3), ("B", HOP_Z6)),
)
MESSAGES = [(stage, name) for stage, hops in enumerate(STAGES) for name, _ in hops]


def group_frequencies():
    p = np.arange(64)
    first = np.concatenate([8 * p, 8 * p + 4])
    return [first] + [8 * np.arange(128) + q for q in (1, 2, 3)]


def split_bf16(x):
    high = x.astype(ml_dtypes.bfloat16)
    low = (x - high.astype(np.float64)).astype(ml_dtypes.bfloat16)
    return high, low


def dft_tables():
    r = np.arange(128)[:, None]
    tables = []
    for at, freqs in enumerate(group_frequencies()):
        angle = 2 * np.pi * ((r * freqs[None, :]) % SEG) / SEG
        cos, sin = np.cos(angle), np.sin(angle)
        if at == 0:
            top = np.concatenate([cos[:, :64], 0 * cos[:, 64:], -sin[:, :64], 0 * sin[:, 64:]], 1)
            top[:, 128] = (-1.0) ** np.arange(128)
            low = np.concatenate([0 * cos[:, :64], cos[:, 64:], 0 * sin[:, :64], -sin[:, 64:]], 1)
        else:
            top = np.concatenate([cos, -sin], 1)
            low = np.concatenate([sin, cos], 1)
        tables.append(np.concatenate([top, low], 0))
    return split_bf16(np.stack(tables))


def lag_table():
    lags = np.arange(LAGS) - LAGS // 2
    rows = []
    for at, freqs in enumerate(group_frequencies()):
        angle = 2 * np.pi * ((freqs[:, None] * lags[None, :]) % SEG) / SEG
        re, im = np.cos(angle) * 2 / SEG, -np.sin(angle) * 2 / SEG
        if at == 0:
            re[0] = 1 / SEG
            im[0] = (-1.0) ** np.abs(lags) / SEG
        rows += [re, im]
    table = np.zeros((GROUPS * 256, 256))
    table[:, :LAGS] = np.concatenate(rows, 0)
    return table.astype(ml_dtypes.bfloat16)


def kernel(
    plan, samples, taps, dft_high, dft_low, lag_mat, self_out, pair_out,
    core_body, hop_body, hold, own_tail, core_tail, hop_tail, hold_tail, send_tail,
    band, xr, xi, yr, yi, yr2, cross, parts, inbox,
    core_sem, tail_sem, ctail_sem, body_sem, htail_sem, red_sem, here_sem,
):
    c = lax.axis_index("chan")
    t = lax.axis_index("tm")

    def chan_peer(hop):
        return (lax.bitwise_xor(c, jnp.int32(hop)), t)

    def tm_peer(d):
        return (c, lax.bitwise_xor(t, jnp.int32(d)))

    barrier = pltpu.get_barrier_semaphore()
    for hop in CHAN_HOPS:
        pl.semaphore_signal(barrier, inc=1, device_id=chan_peer(hop), device_id_type=MESH)
    for d in range(1, TM):
        pl.semaphore_signal(barrier, inc=1, device_id=tm_peer(d), device_id_type=MESH)

    p = [plan[r] for r in range(ROUNDS)]
    free = [jnp.logical_and(m != 1, m != 63) for m in p]
    mask_a = jnp.where(free[0], p[0], jnp.where(free[1], p[1], p[2]))
    mask_b = p[0] + p[1] + p[2] + p[3] - 64 - mask_a

    def flag(m, hop):
        bit = lambda k: (m >> k) & 1
        if hop == HOP_CORE:
            v = bit(0)
        elif hop == HOP_Z1:
            v = bit(1)
        elif hop == HOP_Z6:
            v = bit(3)
        elif hop == HOP_Z2:
            v = bit(2) ^ bit(3)
        elif hop == HOP_Y3:
            v = bit(5)
        else:
            v = bit(4) ^ bit(5)
        return v == 1

    masks = {"A": mask_a, "B": mask_b}

    rolled = pltpu.roll(jnp.broadcast_to(taps[...], (256, 256)), 128, 1, stride=1, stride_axis=0)
    toeplitz = rolled[:, :LANES]
    high = toeplitz.astype(BF16)
    band[:, :LANES] = high
    band[:, LANES:] = (toeplitz - high.astype(F32)).astype(BF16)

    pl.semaphore_wait(barrier, len(CHAN_HOPS) + TM - 1)

    def remote(src, dst, sem, device):
        return pltpu.make_async_remote_copy(
            src_ref=src, dst_ref=dst, send_sem=sem.at[0], recv_sem=sem.at[1],
            device_id=device, device_id_type=MESH,
        )

    core_copy = remote(samples, core_body, core_sem, chan_peer(HOP_CORE))
    core_copy.start()
    send_tail[...] = samples[:, (TILES - 1) * LANES :]
    tail_copy = remote(send_tail, own_tail, tail_sem, (c, lax.rem(t + 1, TM)))
    tail_copy.start()

    body_copies, tail_copies = {}, {}

    def send_bodies(stage):
        for name, hop in STAGES[stage]:
            at = MESSAGES.index((stage, name))
            src = core_body if (stage, name) == (0, "F") else hold.at[at]
            copy = remote(src, hop_body.at[at], body_sem.at[at], chan_peer(hop))
            copy.start()
            body_copies[at] = copy

    def send_tails(stage):
        for name, hop in STAGES[stage]:
            at = MESSAGES.index((stage, name))
            copy = remote(hold_tail.at[at], hop_tail.at[at], htail_sem.at[at], chan_peer(hop))
            copy.start()
            tail_copies[at] = copy

    def last_message(name, stage):
        return [i for i, (s, n) in enumerate(MESSAGES) if n == name and s <= stage][-1]

    def advance(stage, copies, held, arrived):
        later = {}
        for name, hop in STAGES[stage]:
            at = MESSAGES.index((stage, name))
            copies[at].wait_recv()
            if name == "F":
                later[name] = arrived[at]
            else:
                later[name] = jnp.where(flag(masks[name], hop), arrived[at], held[at])
        return later

    def place(values, stage, held):
        for name, value in values.items():
            following = [i for i, (s, n) in enumerate(MESSAGES) if n == name and s > stage]
            slot = following[0] if following else len(MESSAGES) + "ABF".index(name)
            held[slot] = value

    def spectra(body, tail):
        tiles = [body[:, j * LANES : (j + 1) * LANES] for j in range(TILES)]
        now = jnp.concatenate(tiles, 0)
        before = jnp.concatenate([tail] + tiles[:-1], 0)
        both = jnp.dot(jnp.concatenate([before, now], 1), band[...], preferred_element_type=F32)
        filtered = both[:, :LANES] + both[:, LANES:]
        y = []
        for j in range(8):
            y.append(jnp.concatenate(
                [filtered[(s * 8 + j) * CH : (s * 8 + j + 1) * CH] for s in range(2)], 0))
        add = [y[j] + y[j + 4] for j in range(4)]
        sub = [y[j] - y[j + 4] for j in range(4)]
        root = np.float32(np.sqrt(0.5))
        e02, e13 = add[0] + add[2], add[1] + add[3]
        dm, dp = (sub[1] - sub[3]) * root, (sub[1] + sub[3]) * root
        z = (
            (e02 + e13, e02 - e13),
            (sub[0] + dm, -sub[2] - dp),
            (add[0] - add[2], add[3] - add[1]),
            (sub[0] - dm, sub[2] - dp),
        )
        re, im = [], []
        total = None
        for g in range(GROUPS):
            full = jnp.concatenate(z[g], 1)
            z_high = full.astype(BF16)
            z_low = (full - z_high.astype(F32)).astype(BF16)
            first = jnp.dot(jnp.concatenate([z_high, z_low], 0), dft_high[g], preferred_element_type=F32)
            second = jnp.dot(z_high, dft_low[g], preferred_element_type=F32)
            out = first[:32] + (first[32:] + second)
            re.append(out[:, :LANES])
            im.append(out[:, LANES:])
            energy = re[g] * re[g] + im[g] * im[g]
            total = energy if total is None else total + energy
        water = jnp.sum(total, axis=1, keepdims=True) * np.float32(0.1 / 513) + np.float32(1e-6)
        lane0 = lax.broadcasted_iota(jnp.int32, (32, LANES), 1) == 0
        result = []
        for g in range(GROUPS):
            re2, im2 = re[g] * re[g], im[g] * im[g]
            if g == 0:
                inv_re = lax.rsqrt(jnp.where(lane0, re2, re2 + im2) + water)
                inv_im = lax.rsqrt(jnp.where(lane0, im2, re2 + im2) + water)
            else:
                inv_re = inv_im = lax.rsqrt(re2 + im2 + water)
            result.append((
                (re[g] * inv_re).astype(BF16).astype(F32),
                (im[g] * inv_im).astype(BF16).astype(F32),
            ))
        return result

    def keep_partner(spec):
        lane0 = lax.broadcasted_iota(jnp.int32, (32, LANES), 1) == 0
        for g in range(GROUPS):
            re, im = spec[g]
            yr[g] = re
            if g == 0:
                yi[g] = jnp.where(lane0, 0.0, im)
                yr2[g] = jnp.where(lane0, im, re)
            else:
                yi[g] = im
                yr2[g] = re

    def correlate(slot):
        def step(a, carry):
            for g in range(GROUPS):
                sum_re = sum_im = None
                for s in range(2):
                    rows = pl.ds(s * CH, CH)
                    x_re = xr[g, pl.ds(s * CH + a, 1), :]
                    x_im = xi[g, pl.ds(s * CH + a, 1), :]
                    y_im = yi[g, rows, :]
                    term_re = x_re * yr[g, rows, :] + x_im * y_im
                    term_im = x_im * yr2[g, rows, :] - x_re * y_im
                    sum_re = term_re if s == 0 else sum_re + term_re
                    sum_im = term_im if s == 0 else sum_im + term_im
                where = pl.ds(pl.multiple_of(a * CH, CH), CH)
                cross[where, g * 256 : g * 256 + LANES] = sum_re.astype(BF16)
                cross[where, g * 256 + LANES : (g + 1) * 256] = sum_im.astype(BF16)
            return carry

        lax.fori_loop(0, CH, step, 0)
        lagged = jnp.dot(cross[...], lag_mat[...], preferred_element_type=F32)
        parts[slot] = lagged.astype(BF16).reshape(TM, 32, 256)

    reduce_copies = []

    def send_parts(first, count):
        for d in range(1, TM):
            copy = remote(
                parts.at[pl.ds(first, count), lax.bitwise_xor(t, jnp.int32(d))],
                inbox.at[d - 1, pl.ds(first, count)],
                red_sem.at[first, d - 1],
                tm_peer(d),
            )
            copy.start()
            reduce_copies.append(copy)

    core_copy.wait_recv()
    mine, theirs = samples[...], core_body[...]
    place({n: jnp.where(flag(masks[n], HOP_CORE), theirs, mine) for n in "AB"}, -1, hold)
    send_bodies(0)

    tail_copy.wait_recv()
    own_tail[...] = jnp.where(t == 0, jnp.zeros_like(own_tail), own_tail[...])
    core_tail_copy = remote(own_tail, core_tail, ctail_sem, chan_peer(HOP_CORE))
    core_tail_copy.start()

    spec = spectra(mine, own_tail[...])
    for g in range(GROUPS):
        xr[g], xi[g] = spec[g]
    keep_partner(spec)

    core_tail_copy.wait_recv()
    mine, theirs = own_tail[...], core_tail[...]
    values = {n: jnp.where(flag(masks[n], HOP_CORE), theirs, mine) for n in "AB"}
    values["F"] = theirs
    place(values, -1, hold_tail)
    send_tails(0)

    correlate(0)

    def hop_on(stage):
        place(advance(stage, body_copies, hold, hop_body), stage, hold)
        if stage + 1 < len(STAGES):
            send_bodies(stage + 1)
        place(advance(stage, tail_copies, hold_tail, hop_tail), stage, hold_tail)
        if stage + 1 < len(STAGES):
            send_tails(stage + 1)

    hop_on(0)
    keep_partner(spectra(core_body[...], core_tail[...]))
    correlate(1)
    send_parts(0, 2)
    hop_on(1)
    hop_on(2)
    at = len(MESSAGES) + 2
    keep_partner(spectra(hold[at], hold_tail[at]))
    correlate(2)
    send_parts(2, 1)
    hop_on(3)
    hop_on(4)
    for i in range(2):
        at = len(MESSAGES) + i
        keep_partner(spectra(hold[at], hold_tail[at]))
        correlate(3 + i)
        send_parts(3 + i, 1)

    for copy in [core_copy, tail_copy, core_tail_copy, *body_copies.values(), *tail_copies.values()]:
        copy.wait_send()
    for copy in reduce_copies:
        copy.wait_recv()
    sums = []
    for slot in range(5):
        acc = parts[slot, t].astype(F32)
        for d in range(1, TM):
            acc = acc + inbox[d - 1, slot].astype(F32)
        sums.append(acc[:, :LAGS].reshape(2, CH, LAGS))
    self_out[...] = sums[0]
    for r in range(ROUNDS):
        rest = jnp.where(p[r] == mask_a, sums[3], sums[4])
        pair_out[r] = jnp.where(p[r] == 1, sums[1], jnp.where(p[r] == 63, sums[2], rest))
    for copy in reduce_copies:
        copy.wait_send()


def on_device(samples, fir_taps, plan):
    dft_high, dft_low = dft_tables()
    lag_mat = lag_table()
    taps = jnp.pad(fir_taps, (0, 256 - fir_taps.shape[0])).reshape(1, 256)
    vmem = pl.BlockSpec(memory_space=pltpu.VMEM)
    slots = len(MESSAGES) + 3
    n = len(MESSAGES)
    dma = pltpu.SemaphoreType.DMA
    return pl.pallas_call(
        kernel,
        out_shape=(
            jax.ShapeDtypeStruct((2, CH, LAGS), F32),
            jax.ShapeDtypeStruct((ROUNDS, 2, CH, LAGS), F32),
        ),
        in_specs=[pl.BlockSpec(memory_space=pltpu.SMEM)] + [vmem] * 5,
        out_specs=(vmem, vmem),
        scratch_shapes=[
            pltpu.VMEM((CH, 2048), BF16),
            pltpu.VMEM((n, CH, 2048), BF16),
            pltpu.VMEM((slots, CH, 2048), BF16),
            pltpu.VMEM((CH, LANES), BF16),
            pltpu.VMEM((CH, LANES), BF16),
            pltpu.VMEM((n, CH, LANES), BF16),
            pltpu.VMEM((slots, CH, LANES), BF16),
            pltpu.VMEM((CH, LANES), BF16),
            pltpu.VMEM((256, 256), BF16),
            pltpu.VMEM((GROUPS, 32, LANES), F32),
            pltpu.VMEM((GROUPS, 32, LANES), F32),
            pltpu.VMEM((GROUPS, 32, LANES), F32),
            pltpu.VMEM((GROUPS, 32, LANES), F32),
            pltpu.VMEM((GROUPS, 32, LANES), F32),
            pltpu.VMEM((256, GROUPS * 256), BF16),
            pltpu.VMEM((5, TM, 32, 256), BF16),
            pltpu.VMEM((TM - 1, 5, 32, 256), BF16),
            dma((2,)),
            dma((2,)),
            dma((2,)),
            dma((n, 2)),
            dma((n, 2)),
            dma((5, TM - 1, 2)),
            pltpu.SemaphoreType.REGULAR,
        ],
        compiler_params=pltpu.CompilerParams(
            collective_id=0, has_side_effects=True, vmem_limit_bytes=48 * 1024 * 1024
        ),
        cost_estimate=pl.CostEstimate(flops=10**9, bytes_accessed=4 * 10**6, transcendentals=10**5),
        name="correlate_blocks",
    )(plan, samples, taps, jnp.asarray(dft_high), jnp.asarray(dft_low), jnp.asarray(lag_mat))


def solution(mesh):
    in_specs = (P("chan", "tm"), P(), P())
    out_specs = (P(("chan", "tm"), None, None), P(None, ("chan", "tm"), None, None))
    return jax.shard_map(
        on_device, mesh=mesh, in_specs=in_specs, out_specs=out_specs, check_vma=False
    )
```

```python
import functools

import jax
import jax.numpy as jnp
import ml_dtypes
import numpy as np
from jax import lax
from jax.experimental import pallas as pl
from jax.experimental.pallas import tpu as pltpu
from jax.sharding import PartitionSpec as P

MESH = pl.DeviceIdType.MESH
BF16 = jnp.bfloat16
F32 = jnp.float32

CH = 16
SEG = 1024
LAGS = 129
ROUNDS = 4
TM = 8
LANES = 128
TILES = 16
CHUNKS = 4
WIDTH = 2048 // CHUNKS
GROUPS = 4
HOP_CORE, HOP_Z1, HOP_Z2, HOP_Z6, HOP_Z7, HOP_Y1, HOP_Y3 = 1, 2, 4, 12, 14, 16, 48
CHAN_HOPS = (HOP_CORE, HOP_Z1, HOP_Z2, HOP_Z6, HOP_Z7, HOP_Y1, HOP_Y3)
STAGES = (
    (("A", HOP_Z1), ("B", HOP_Y1)),
    (("A", HOP_Z2), ("B", HOP_Y3), ("F", HOP_Z7)),
    (("A", HOP_Z6), ("B", HOP_Z1), ("F", HOP_Y3)),
    (("A", HOP_Y1), ("B", HOP_Z2)),
    (("A", HOP_Y3), ("B", HOP_Z6)),
)
MESSAGES = [(stage, name) for stage, hops in enumerate(STAGES) for name, _ in hops]
FIRST_F = [m for m in MESSAGES if m[1] == "F"][0]


def group_frequencies():
    p = np.arange(64)
    first = np.concatenate([8 * p, 8 * p + 4])
    return [first] + [8 * np.arange(128) + q for q in (1, 2, 3)]


def split_bf16(x):
    high = x.astype(ml_dtypes.bfloat16)
    low = (x - high.astype(np.float64)).astype(ml_dtypes.bfloat16)
    return high, low


def dft_tables():
    r = np.arange(128)[:, None]
    tables = []
    for at, freqs in enumerate(group_frequencies()):
        angle = 2 * np.pi * ((r * freqs[None, :]) % SEG) / SEG
        cos, sin = np.cos(angle), np.sin(angle)
        if at == 0:
            top = np.concatenate([cos[:, :64], 0 * cos[:, 64:], -sin[:, :64], 0 * sin[:, 64:]], 1)
            top[:, 128] = (-1.0) ** np.arange(128)
            low = np.concatenate([0 * cos[:, :64], cos[:, 64:], 0 * sin[:, :64], -sin[:, 64:]], 1)
        else:
            top = np.concatenate([cos, -sin], 1)
            low = np.concatenate([sin, cos], 1)
        tables.append(np.concatenate([top, low], 0))
    return split_bf16(np.stack(tables))


def lag_table():
    lags = np.arange(LAGS) - LAGS // 2
    rows = []
    for at, freqs in enumerate(group_frequencies()):
        angle = 2 * np.pi * ((freqs[:, None] * lags[None, :]) % SEG) / SEG
        re, im = np.cos(angle) * 2 / SEG, -np.sin(angle) * 2 / SEG
        if at == 0:
            re[0] = 1 / SEG
            im[0] = (-1.0) ** np.abs(lags) / SEG
        rows += [re, im]
    table = np.zeros((GROUPS * 256, 256))
    table[:, :LAGS] = np.concatenate(rows, 0)
    return table.astype(ml_dtypes.bfloat16)


def known(mask):
    return jnp.logical_or(mask == 1, mask == 63)


def kernel(
    plan_in, samples, taps_in, dft_high_in, dft_low_in, lag_in, sums,
    plan, taps, taps_row, dft_high, dft_low, lag_mat, own_body, core_body, hop_body, hold,
    own_tail, core_tail, hop_tail, hold_tail,
    band, xr, xi, yr, yi, yr2, cross, parts, inbox,
    load_sem, core_sem, tail_sem, body_sem, htail_sem, red_sem,
):
    c = lax.axis_index("chan")
    t = lax.axis_index("tm")

    def chan_peer(hop):
        return (lax.bitwise_xor(c, jnp.int32(hop)), t)

    def tm_peer(d):
        return (c, lax.bitwise_xor(t, jnp.int32(d)))

    later, earlier = lax.rem(t + 1, TM), lax.rem(t + TM - 1, TM)
    other = lax.bitwise_xor(c, jnp.int32(HOP_CORE))

    barrier = pltpu.get_barrier_semaphore()
    greeted = [chan_peer(hop) for hop in CHAN_HOPS] + [tm_peer(d) for d in range(1, TM)]
    greeted += [(other, later), (other, earlier)]
    for device in greeted:
        pl.semaphore_signal(barrier, inc=1, device_id=device, device_id_type=MESH)

    loads = [
        pltpu.make_async_copy(src, dst, load_sem.at[i])
        for i, (src, dst) in enumerate((
            (plan_in, plan), (taps_in, taps), (samples, own_body),
            (dft_high_in, dft_high), (dft_low_in, dft_low), (lag_in, lag_mat),
        ))
    ]
    for load in loads:
        load.start()
    loads[0].wait()
    loads[1].wait()

    p = [plan[r] for r in range(ROUNDS)]
    mask_a = jnp.where(known(p[0]), jnp.where(known(p[1]), p[2], p[1]), p[0])
    mask_b = p[0] + p[1] + p[2] + p[3] - 64 - mask_a
    masks = {"A": mask_a, "B": mask_b}

    def flag(m, hop):
        bit = lambda k: (m >> k) & 1
        if hop == HOP_CORE:
            v = bit(0)
        elif hop == HOP_Z1:
            v = bit(1)
        elif hop == HOP_Z6:
            v = bit(3)
        elif hop == HOP_Z2:
            v = bit(2) ^ bit(3)
        elif hop == HOP_Y3:
            v = bit(5)
        else:
            v = bit(4) ^ bit(5)
        return v == 1

    taps_row[...] = jnp.zeros_like(taps_row)
    taps_row[:, : taps.shape[1]] = taps[...]
    rolled = pltpu.roll(jnp.broadcast_to(taps_row[...], (256, 256)), 128, 1, stride=1, stride_axis=0)
    toeplitz = rolled[:, :LANES]
    high = toeplitz.astype(BF16)
    band[:, :LANES] = high
    band[:, LANES:] = (toeplitz - high.astype(F32)).astype(BF16)
    loads[2].wait()

    pl.semaphore_wait(barrier, len(greeted))

    def remote(src, dst, sem, device):
        return pltpu.make_async_remote_copy(
            src_ref=src, dst_ref=dst, send_sem=sem.at[0], recv_sem=sem.at[1],
            device_id=device, device_id_type=MESH,
        )

    def lanes(h):
        return slice(h * WIDTH, (h + 1) * WIDTH)

    core_copies = []
    for h in range(CHUNKS):
        copy = remote(own_body.at[:, lanes(h)], core_body.at[:, lanes(h)], core_sem.at[h], chan_peer(HOP_CORE))
        copy.start()
        core_copies.append(copy)
    end = own_body.at[:, (TILES - 1) * LANES :]
    tail_copies = [
        remote(end, own_tail, tail_sem.at[0], (c, later)),
        remote(end, core_tail, tail_sem.at[1], (other, later)),
    ]
    for copy in tail_copies:
        copy.start()

    body_hops, tail_hops = {}, {}
    finals = {"A": len(MESSAGES), "B": len(MESSAGES) + 1, "F": len(MESSAGES) + 2}

    def next_slot(name, stage):
        following = [i for i, (s, n) in enumerate(MESSAGES) if n == name and s > stage]
        return following[0] if following else finals[name]

    def send_body(at, h):
        if at < len(MESSAGES):
            stage, name = MESSAGES[at]
            src = core_body if (stage, name) == FIRST_F else hold.at[at]
            copy = remote(
                src.at[:, lanes(h)], hop_body.at[at, :, lanes(h)], body_sem.at[at, h],
                chan_peer(dict(STAGES[stage])[name]),
            )
            copy.start()
            body_hops[at, h] = copy

    def send_tail(at):
        if at < len(MESSAGES):
            stage, name = MESSAGES[at]
            copy = remote(
                hold_tail.at[at], hop_tail.at[at], htail_sem.at[at], chan_peer(dict(STAGES[stage])[name])
            )
            copy.start()
            tail_hops[at] = copy

    def hop_bodies(stage):
        for h in range(CHUNKS):
            for name, hop in STAGES[stage]:
                at = MESSAGES.index((stage, name))
                slot = next_slot(name, stage)
                body_hops[at, h].wait_recv()
                value = hop_body[at, :, lanes(h)]
                if name != "F":
                    value = jnp.where(flag(masks[name], hop), value, hold[at, :, lanes(h)])
                hold[slot, :, lanes(h)] = value
                send_body(slot, h)

    def hop_tails(stage):
        for name, hop in STAGES[stage]:
            at = MESSAGES.index((stage, name))
            slot = next_slot(name, stage)
            tail_hops[at].wait_recv()
            value = hop_tail[at]
            if name != "F":
                value = jnp.where(flag(masks[name], hop), value, hold_tail[at])
            hold_tail[slot] = value
            send_tail(slot)

    def spectra(blocks):
        filtered = []
        for body, tail in blocks:
            tiles = [body[:, j * LANES : (j + 1) * LANES] for j in range(TILES)]
            now = jnp.concatenate(tiles, 0)
            before = jnp.concatenate([tail] + tiles[:-1], 0)
            both = jnp.dot(jnp.concatenate([before, now], 1), band[...], preferred_element_type=F32)
            filtered.append(both[:, :LANES] + both[:, LANES:])
        y = []
        for j in range(8):
            y.append(jnp.concatenate(
                [f[(s * 8 + j) * CH : (s * 8 + j + 1) * CH] for f in filtered for s in range(2)], 0))
        count = 32 * len(blocks)
        add = [y[j] + y[j + 4] for j in range(4)]
        sub = [y[j] - y[j + 4] for j in range(4)]
        root = np.float32(np.sqrt(0.5))
        e02, e13 = add[0] + add[2], add[1] + add[3]
        dm, dp = (sub[1] - sub[3]) * root, (sub[1] + sub[3]) * root
        z = (
            (e02 + e13, e02 - e13),
            (sub[0] + dm, -sub[2] - dp),
            (add[0] - add[2], add[3] - add[1]),
            (sub[0] - dm, sub[2] - dp),
        )
        re, im = [], []
        total = None
        for g in range(GROUPS):
            full = jnp.concatenate(z[g], 1)
            z_high = full.astype(BF16)
            z_low = (full - z_high.astype(F32)).astype(BF16)
            first = jnp.dot(jnp.concatenate([z_high, z_low], 0), dft_high[g], preferred_element_type=F32)
            second = jnp.dot(z_high, dft_low[g], preferred_element_type=F32)
            out = first[:count] + (first[count:] + second)
            re.append(out[:, :LANES])
            im.append(out[:, LANES:])
            energy = re[g] * re[g] + im[g] * im[g]
            total = energy if total is None else total + energy
        water = jnp.sum(total, axis=1, keepdims=True) * np.float32(0.1 / 513) + np.float32(1e-6)
        lane0 = lax.broadcasted_iota(jnp.int32, (count, LANES), 1) == 0
        result = []
        for g in range(GROUPS):
            re2, im2 = re[g] * re[g], im[g] * im[g]
            if g == 0:
                inv_re = lax.rsqrt(jnp.where(lane0, re2, re2 + im2) + water)
                inv_im = lax.rsqrt(jnp.where(lane0, im2, re2 + im2) + water)
            else:
                inv_re = inv_im = lax.rsqrt(re2 + im2 + water)
            result.append((
                (re[g] * inv_re).astype(BF16).astype(F32),
                (im[g] * inv_im).astype(BF16).astype(F32),
            ))
        return result

    def keep_partner(spec, block):
        rows = slice(block * 32, block * 32 + 32)
        lane0 = lax.broadcasted_iota(jnp.int32, (32, LANES), 1) == 0
        for g in range(GROUPS):
            re, im = spec[g][0][rows], spec[g][1][rows]
            yr[g] = re
            if g == 0:
                yi[g] = jnp.where(lane0, 0.0, im)
                yr2[g] = jnp.where(lane0, im, re)
            else:
                yi[g] = im
                yr2[g] = re

    def correlate(slot):
        def step(a, carry):
            for g in range(GROUPS):
                sum_re = sum_im = None
                for s in range(2):
                    rows = pl.ds(s * CH, CH)
                    x_re = xr[g, pl.ds(s * CH + a, 1), :]
                    x_im = xi[g, pl.ds(s * CH + a, 1), :]
                    y_im = yi[g, rows, :]
                    term_re = x_re * yr[g, rows, :] + x_im * y_im
                    term_im = x_im * yr2[g, rows, :] - x_re * y_im
                    sum_re = term_re if s == 0 else sum_re + term_re
                    sum_im = term_im if s == 0 else sum_im + term_im
                where = pl.ds(pl.multiple_of(a * CH, CH), CH)
                cross[where, g * 256 : g * 256 + LANES] = sum_re.astype(BF16)
                cross[where, g * 256 + LANES : (g + 1) * 256] = sum_im.astype(BF16)
            return carry

        lax.fori_loop(0, CH, step, 0)
        lagged = jnp.dot(cross[...], lag_mat[...], preferred_element_type=F32)
        parts[slot] = lagged.astype(BF16).reshape(TM, 32, 256)

    reduce_copies = []

    def send_parts(first, count):
        for d in range(1, TM):
            copy = remote(
                parts.at[pl.ds(first, count), lax.bitwise_xor(t, jnp.int32(d))],
                inbox.at[d - 1, pl.ds(first, count)],
                red_sem.at[first, d - 1],
                tm_peer(d),
            )
            copy.start()
            reduce_copies.append(copy)

    for h in range(CHUNKS):
        core_copies[h].wait_recv()
        mine, theirs = own_body[:, lanes(h)], core_body[:, lanes(h)]
        for n in "AB":
            at = next_slot(n, -1)
            hold[at, :, lanes(h)] = jnp.where(flag(masks[n], HOP_CORE), theirs, mine)
            send_body(at, h)
        send_body(next_slot("F", -1), h)
    for load in loads[3:]:
        load.wait()

    hop_bodies(0)
    for copy in tail_copies:
        copy.wait_recv()
    mine = jnp.where(t == 0, jnp.zeros_like(own_tail), own_tail[...])
    theirs = jnp.where(t == 0, jnp.zeros_like(core_tail), core_tail[...])
    for n in "ABF":
        at = next_slot(n, -1)
        hold_tail[at] = theirs if n == "F" else jnp.where(flag(masks[n], HOP_CORE), theirs, mine)
        send_tail(at)
    spec = spectra([(own_body[...], mine), (core_body[...], theirs)])
    for g in range(GROUPS):
        xr[g], xi[g] = spec[g][0][:32], spec[g][1][:32]
    keep_partner(spec, 0)
    correlate(0)
    hop_tails(0)
    hop_bodies(1)
    keep_partner(spec, 1)
    correlate(1)
    send_parts(0, 2)
    hop_tails(1)
    hop_bodies(2)
    hop_tails(2)
    spec = spectra([(hold[finals["F"]], hold_tail[finals["F"]])])
    keep_partner(spec, 0)
    correlate(2)
    send_parts(2, 1)
    hop_bodies(3)
    hop_tails(3)
    hop_bodies(4)
    hop_tails(4)
    spec = spectra([(hold[finals[n]], hold_tail[finals[n]]) for n in "AB"])
    for i in range(2):
        keep_partner(spec, i)
        correlate(3 + i)
        send_parts(3 + i, 1)

    for copy in [*core_copies, *tail_copies, *body_hops.values(), *tail_hops.values()]:
        copy.wait_send()
    for copy in reduce_copies:
        copy.wait_recv()
    for slot in range(5):
        acc = parts[slot, t].astype(F32)
        for d in range(1, TM):
            acc = acc + inbox[d - 1, slot].astype(F32)
        sums[slot] = acc
    for copy in reduce_copies:
        copy.wait_send()


def hand_out(plan, sums, self_out, pair_out):
    p = [plan[r] for r in range(ROUNDS)]
    first = jnp.where(known(p[0]), jnp.where(known(p[1]), p[2], p[1]), p[0])
    shaped = lambda i: sums[i][:, :LAGS].reshape(2, CH, LAGS)
    self_out[...] = shaped(0)
    for r in range(ROUNDS):
        slot = jnp.where(p[r] == 1, 1, jnp.where(p[r] == 63, 2, jnp.where(p[r] == first, 3, 4)))
        pair_out[r] = shaped(slot)


def on_device(samples, fir_taps, plan):
    dft_high, dft_low = dft_tables()
    lag_mat = lag_table()
    vmem = pl.BlockSpec(memory_space=pltpu.VMEM)
    anywhere = pl.BlockSpec(memory_space=pl.ANY)
    n = len(MESSAGES)
    slots = n + 3
    dma = pltpu.SemaphoreType.DMA
    taps = fir_taps.reshape(1, -1)
    sums = pl.pallas_call(
        kernel,
        out_shape=jax.ShapeDtypeStruct((5, 32, 256), F32),
        in_specs=[anywhere] * 6,
        out_specs=vmem,
        scratch_shapes=[
            pltpu.SMEM((ROUNDS,), jnp.int32),
            pltpu.VMEM(taps.shape, F32),
            pltpu.VMEM((1, 256), F32),
            pltpu.VMEM(dft_high.shape, BF16),
            pltpu.VMEM(dft_low.shape, BF16),
            pltpu.VMEM(lag_mat.shape, BF16),
            pltpu.VMEM((CH, 2048), BF16),
            pltpu.VMEM((CH, 2048), BF16),
            pltpu.VMEM((n, CH, 2048), BF16),
            pltpu.VMEM((slots, CH, 2048), BF16),
            pltpu.VMEM((CH, LANES), BF16),
            pltpu.VMEM((CH, LANES), BF16),
            pltpu.VMEM((n, CH, LANES), BF16),
            pltpu.VMEM((slots, CH, LANES), BF16),
            pltpu.VMEM((256, 256), BF16),
            pltpu.VMEM((GROUPS, 32, LANES), F32),
            pltpu.VMEM((GROUPS, 32, LANES), F32),
            pltpu.VMEM((GROUPS, 32, LANES), F32),
            pltpu.VMEM((GROUPS, 32, LANES), F32),
            pltpu.VMEM((GROUPS, 32, LANES), F32),
            pltpu.VMEM((256, GROUPS * 256), BF16),
            pltpu.VMEM((5, TM, 32, 256), BF16),
            pltpu.VMEM((TM - 1, 5, 32, 256), BF16),
            dma((6,)),
            dma((CHUNKS, 2)),
            dma((2, 2)),
            dma((n, CHUNKS, 2)),
            dma((n, 2)),
            dma((5, TM - 1, 2)),
        ],
        compiler_params=pltpu.CompilerParams(
            collective_id=0, has_side_effects=True, vmem_limit_bytes=62 * 1024 * 1024
        ),
        cost_estimate=pl.CostEstimate(flops=10**9, bytes_accessed=4 * 10**6, transcendentals=10**5),
        name="correlate_blocks",
    )(plan, samples, taps, jnp.asarray(dft_high), jnp.asarray(dft_low), jnp.asarray(lag_mat))
    return pl.pallas_call(
        hand_out,
        out_shape=(
            jax.ShapeDtypeStruct((2, CH, LAGS), F32),
            jax.ShapeDtypeStruct((ROUNDS, 2, CH, LAGS), F32),
        ),
        in_specs=[pl.BlockSpec(memory_space=pltpu.SMEM), vmem],
        out_specs=(vmem, vmem),
        cost_estimate=pl.CostEstimate(flops=0, bytes_accessed=5 * 10**5, transcendentals=0),
        name="hand_out_rounds",
    )(plan, sums)


def solution(mesh):
    in_specs = (P("chan", "tm"), P(), P())
    out_specs = (P(("chan", "tm"), None, None), P(None, ("chan", "tm"), None, None))
    return jax.shard_map(
        on_device, mesh=mesh, in_specs=in_specs, out_specs=out_specs, check_vma=False
    )
```

```python
import functools

import jax
import jax.numpy as jnp
import ml_dtypes
import numpy as np
from jax import lax
from jax.experimental import pallas as pl
from jax.experimental.pallas import tpu as pltpu
from jax.sharding import PartitionSpec as P

MESH = pl.DeviceIdType.MESH
BF16 = jnp.bfloat16
F32 = jnp.float32

CH = 16
SEG = 1024
LAGS = 129
ROUNDS = 4
TM = 8
LANES = 128
TILES = 16
CHUNKS = 4
WIDTH = 2048 // CHUNKS
ROWS = 48
GROUPS = 4
HOP_CORE, HOP_Z1, HOP_Z2, HOP_Z6, HOP_Z7, HOP_Y1, HOP_Y3 = 1, 2, 4, 12, 14, 16, 48
CHAN_HOPS = (HOP_CORE, HOP_Z1, HOP_Z1 ^ HOP_CORE, HOP_Z2, HOP_Z6, HOP_Z7, HOP_Y1, HOP_Y3)
STAGES = (
    (("A", HOP_Z2), ("B", HOP_Y3), ("F", HOP_Z7)),
    (("A", HOP_Z6), ("B", HOP_Y1), ("F", HOP_Y3)),
    (("A", HOP_Y1), ("B", HOP_Z6)),
    (("A", HOP_Y3), ("B", HOP_Z2)),
)
FLAGGED = (HOP_CORE, HOP_Z1, HOP_Z2, HOP_Z6, HOP_Y1, HOP_Y3)
NEAR = (HOP_CORE, HOP_Z1, HOP_Z1 ^ HOP_CORE)


def messages(stages):
    return [(stage, name, hop) for stage, hops in enumerate(stages) for name, hop in hops]


def group_frequencies():
    p = np.arange(64)
    first = np.concatenate([8 * p, 8 * p + 4])
    return [first] + [8 * np.arange(128) + q for q in (1, 2, 3)]


def split_bf16(x):
    high = x.astype(ml_dtypes.bfloat16)
    low = (x - high.astype(np.float64)).astype(ml_dtypes.bfloat16)
    return high, low


def dft_tables():
    r = np.arange(128)[:, None]
    tables = []
    for at, freqs in enumerate(group_frequencies()):
        angle = 2 * np.pi * ((r * freqs[None, :]) % SEG) / SEG
        cos, sin = np.cos(angle), np.sin(angle)
        if at == 0:
            top = np.concatenate([cos[:, :64], 0 * cos[:, 64:], -sin[:, :64], 0 * sin[:, 64:]], 1)
            top[:, 128] = (-1.0) ** np.arange(128)
            low = np.concatenate([0 * cos[:, :64], cos[:, 64:], 0 * sin[:, :64], -sin[:, 64:]], 1)
        else:
            top = np.concatenate([cos, -sin], 1)
            low = np.concatenate([sin, cos], 1)
        tables.append(np.concatenate([top, low], 0))
    return split_bf16(np.stack(tables))


def lag_table():
    lags = np.arange(LAGS) - LAGS // 2
    rows = []
    for at, freqs in enumerate(group_frequencies()):
        angle = 2 * np.pi * ((freqs[:, None] * lags[None, :]) % SEG) / SEG
        re, im = np.cos(angle) * 2 / SEG, -np.sin(angle) * 2 / SEG
        if at == 0:
            re[0] = 1 / SEG
            im[0] = (-1.0) ** np.abs(lags) / SEG
        rows += [re, im]
    table = np.zeros((GROUPS * 256, 256))
    table[:, :LAGS] = np.concatenate(rows, 0)
    table[:, LAGS] = table[:, LAGS - 1]
    return table.astype(ml_dtypes.bfloat16)


def known(mask):
    return jnp.logical_or(mask == 1, mask == 63)


class Stream:
    def __init__(self, stages, pieces, flags, held, arrived, sems, send):
        self.pieces, self.flags = pieces, flags
        self.held, self.arrived, self.sems, self.send = held, arrived, sems, send
        self.order = messages(stages)
        self.finals = {n: len(self.order) + k for k, n in enumerate("ABF")}
        self.copies = {}

    def slot(self, name, stage=-1):
        following = [k for k, (at, n, _) in enumerate(self.order) if n == name and at > stage]
        return following[0] if following else self.finals[name]

    def leave(self, at, h, source=None):
        if at < len(self.order):
            piece = self.pieces[h]
            source = self.held.at[at] if source is None else source
            copy = self.send(
                source.at[:, piece], self.arrived.at[at, :, piece], self.sems.at[at, h], self.order[at][2]
            )
            copy.start()
            self.copies[at, h] = copy

    def hop(self, stage):
        for h, piece in enumerate(self.pieces):
            for at, (when, name, hop) in enumerate(self.order):
                if when == stage:
                    self.copies[at, h].wait_recv()
                    value = self.arrived[at, :, piece]
                    if name != "F":
                        value = jnp.where(self.flags[name, hop], value, self.held[at, :, piece])
                    after = self.slot(name, stage)
                    self.held[after, :, piece] = value
                    self.leave(after, h)


def kernel(
    plan_in, samples, taps_in, dft_high_in, dft_low_in, lag_in, sums,
    plan, taps, taps_row, dft_high, dft_low, lag_mat, own, near_body, hop_body, hold,
    near_tails, hop_tail, hold_tail,
    band, xr, xi, yr, yi, yr2, cross, parts, inbox,
    load_sem, first_sem, near_sem, body_sem, tail_sem, red_sem,
):
    c = lax.axis_index("chan")
    t = lax.axis_index("tm")

    def chan_peer(hop):
        return (lax.bitwise_xor(c, jnp.int32(hop)), t)

    def tm_peer(d):
        return (c, lax.bitwise_xor(t, jnp.int32(d)))

    later, earlier = lax.rem(t + 1, TM), lax.rem(t + TM - 1, TM)

    barrier = pltpu.get_barrier_semaphore()
    greeted = [chan_peer(hop) for hop in CHAN_HOPS] + [tm_peer(d) for d in range(1, TM)]
    greeted += [(chan_peer(hop)[0], side) for hop in NEAR for side in (later, earlier)]
    for device in greeted:
        pl.semaphore_signal(barrier, inc=1, device_id=device, device_id_type=MESH)

    loads = [
        pltpu.make_async_copy(src, dst, load_sem.at[i])
        for i, (src, dst) in enumerate((
            (plan_in, plan), (taps_in, taps), (samples, own),
            (dft_high_in, dft_high), (dft_low_in, dft_low), (lag_in, lag_mat),
        ))
    ]
    for load in loads:
        load.start()
    pl.semaphore_wait(barrier, len(greeted))

    def remote(src, dst, sem, device):
        return pltpu.make_async_remote_copy(
            src_ref=src, dst_ref=dst, send_sem=sem.at[0], recv_sem=sem.at[1],
            device_id=device, device_id_type=MESH,
        )

    def by_hop(src, dst, sem, hop):
        return remote(src, dst, sem, chan_peer(hop))

    pieces = [slice(h * WIDTH, (h + 1) * WIDTH) for h in range(CHUNKS)]
    first_copies = [
        [by_hop(samples.at[:, piece], near_body.at[k, :, piece], first_sem.at[h, k], hop) for k, hop in enumerate(NEAR)]
        for h, piece in enumerate(pieces)
    ]
    end = samples.at[:, (TILES - 1) * LANES :]
    near_copies = [
        remote(end, near_tails.at[k], near_sem.at[k], (chan_peer(hop)[0], later))
        for k, hop in enumerate((0,) + NEAR)
    ]
    for copy in [*first_copies[0], *near_copies, *sum(first_copies[1:], [])]:
        copy.start()

    loads[0].wait()
    loads[1].wait()

    p = [plan[r] for r in range(ROUNDS)]
    mask_a = jnp.where(known(p[0]), jnp.where(known(p[1]), p[2], p[1]), p[0])
    mask_b = p[0] + p[1] + p[2] + p[3] - 64 - mask_a

    def flag(m, hop):
        bit = lambda k: (m >> k) & 1
        if hop == HOP_CORE:
            v = bit(0)
        elif hop == HOP_Z1:
            v = bit(1)
        elif hop == HOP_Z6:
            v = bit(3)
        elif hop == HOP_Z2:
            v = bit(2) ^ bit(3)
        elif hop == HOP_Y3:
            v = bit(5)
        else:
            v = bit(4) ^ bit(5)
        return v == 1

    flags = {(n, hop): flag(m, hop) for n, m in (("A", mask_a), ("B", mask_b)) for hop in FLAGGED}

    taps_row[...] = jnp.zeros_like(taps_row)
    taps_row[:, : taps.shape[1]] = taps[...]
    rolled = pltpu.roll(jnp.broadcast_to(taps_row[...], (256, 256)), 128, 1, stride=1, stride_axis=0)
    toeplitz = rolled[:, :LANES]
    high = toeplitz.astype(BF16)
    band[:, :LANES] = high
    band[:, LANES:] = (toeplitz - high.astype(F32)).astype(BF16)
    body = Stream(STAGES, pieces, flags, hold, hop_body, body_sem, by_hop)
    tail = Stream(STAGES, [slice(0, LANES)], flags, hold_tail, hop_tail, tail_sem, by_hop)

    def choose(name, values):
        core, z1 = flags[name, HOP_CORE], flags[name, HOP_Z1]
        return jnp.where(z1, jnp.where(core, values[3], values[2]), jnp.where(core, values[1], values[0]))

    def spectra(blocks):
        filtered = []
        for block, before_it in blocks:
            tiles = [block[:, j * LANES : (j + 1) * LANES] for j in range(TILES)]
            now = jnp.concatenate(tiles, 0)
            before = jnp.concatenate([before_it] + tiles[:-1], 0)
            both = jnp.dot(jnp.concatenate([before, now], 1), band[...], preferred_element_type=F32)
            filtered.append(both[:, :LANES] + both[:, LANES:])
        y = []
        for j in range(8):
            y.append(jnp.concatenate(
                [f[(s * 8 + j) * CH : (s * 8 + j + 1) * CH] for f in filtered for s in range(2)], 0))
        count = 32 * len(blocks)
        add = [y[j] + y[j + 4] for j in range(4)]
        sub = [y[j] - y[j + 4] for j in range(4)]
        root = np.float32(np.sqrt(0.5))
        e02, e13 = add[0] + add[2], add[1] + add[3]
        dm, dp = (sub[1] - sub[3]) * root, (sub[1] + sub[3]) * root
        z = (
            (e02 + e13, e02 - e13),
            (sub[0] + dm, -sub[2] - dp),
            (add[0] - add[2], add[3] - add[1]),
            (sub[0] - dm, sub[2] - dp),
        )
        re, im = [], []
        total = None
        for g in range(GROUPS):
            full = jnp.concatenate(z[g], 1)
            z_high = full.astype(BF16)
            z_low = (full - z_high.astype(F32)).astype(BF16)
            first = jnp.dot(jnp.concatenate([z_high, z_low], 0), dft_high[g], preferred_element_type=F32)
            second = jnp.dot(z_high, dft_low[g], preferred_element_type=F32)
            out = first[:count] + (first[count:] + second)
            re.append(out[:, :LANES])
            im.append(out[:, LANES:])
            energy = re[g] * re[g] + im[g] * im[g]
            total = energy if total is None else total + energy
        water = jnp.sum(total, axis=1, keepdims=True) * np.float32(0.1 / 513) + np.float32(1e-6)
        lane0 = lax.broadcasted_iota(jnp.int32, (count, LANES), 1) == 0
        result = []
        for g in range(GROUPS):
            re2, im2 = re[g] * re[g], im[g] * im[g]
            if g == 0:
                inv_re = lax.rsqrt(jnp.where(lane0, re2, re2 + im2) + water)
                inv_im = lax.rsqrt(jnp.where(lane0, im2, re2 + im2) + water)
            else:
                inv_re = inv_im = lax.rsqrt(re2 + im2 + water)
            result.append((
                (re[g] * inv_re).astype(BF16).astype(F32),
                (im[g] * inv_im).astype(BF16).astype(F32),
            ))
        return result

    def keep_partner(spec, block):
        rows = slice(block * 32, block * 32 + 32)
        lane0 = lax.broadcasted_iota(jnp.int32, (32, LANES), 1) == 0
        for g in range(GROUPS):
            re, im = spec[g][0][rows], spec[g][1][rows]
            yr[g] = re
            if g == 0:
                yi[g] = jnp.where(lane0, 0.0, im)
                yr2[g] = jnp.where(lane0, im, re)
            else:
                yi[g] = im
                yr2[g] = re

    def correlate(slot):
        def step(a, carry):
            for g in range(GROUPS):
                sum_re = sum_im = None
                for s in range(2):
                    rows = pl.ds(s * CH, CH)
                    x_re = xr[g, pl.ds(s * CH + a, 1), :]
                    x_im = xi[g, pl.ds(s * CH + a, 1), :]
                    y_im = yi[g, rows, :]
                    term_re = x_re * yr[g, rows, :] + x_im * y_im
                    term_im = x_im * yr2[g, rows, :] - x_re * y_im
                    sum_re = term_re if s == 0 else sum_re + term_re
                    sum_im = term_im if s == 0 else sum_im + term_im
                where = pl.ds(pl.multiple_of(a * CH, CH), CH)
                cross[where, g * 256 : g * 256 + LANES] = sum_re.astype(BF16)
                cross[where, g * 256 + LANES : (g + 1) * 256] = sum_im.astype(BF16)
            return carry

        lax.fori_loop(0, CH, step, 0)
        lagged = jnp.dot(cross[...], lag_mat[...], preferred_element_type=F32)
        parts[slot, :, :32, :] = lagged[:, :LANES].astype(BF16).reshape(TM, 32, LANES)
        last = lagged[:, LANES:].reshape(TM, 2, CH, LANES)
        lane0 = lax.broadcasted_iota(jnp.int32, (TM, CH, LANES), 2) == 0
        parts[slot, :, 32:, :] = jnp.where(lane0, last[:, 0], last[:, 1]).astype(BF16)

    reduce_copies = []

    def send_parts(first, count):
        for d in range(1, TM):
            copy = remote(
                parts.at[pl.ds(first, count), lax.bitwise_xor(t, jnp.int32(d))],
                inbox.at[d - 1, pl.ds(first, count)],
                red_sem.at[first, d - 1],
                tm_peer(d),
            )
            copy.start()
            reduce_copies.append(copy)

    for load in loads[2:]:
        load.wait()
    for h, piece in enumerate(pieces):
        for copy in first_copies[h]:
            copy.wait_recv()
        blocks = [own[:, piece]] + [near_body[k, :, piece] for k in range(len(NEAR))]
        for n in "AB":
            hold[body.slot(n), :, piece] = choose(n, blocks)
            body.leave(body.slot(n), h)
        body.leave(body.slot("F"), h, near_body.at[0])

    for copy in near_copies[:2]:
        copy.wait_recv()
    ends = [jnp.where(t == 0, jnp.zeros((CH, LANES), BF16), near_tails[k]) for k in range(2)]
    hold_tail[tail.slot("F")] = ends[1]
    tail.leave(tail.slot("F"), 0)
    spec = spectra([(own[...], ends[0]), (near_body[0], ends[1])])
    for g in range(GROUPS):
        xr[g], xi[g] = spec[g][0][:32], spec[g][1][:32]

    for copy in near_copies[2:]:
        copy.wait_recv()
    ends += [jnp.where(t == 0, jnp.zeros((CH, LANES), BF16), near_tails[k]) for k in (2, 3)]
    for n in "AB":
        hold_tail[tail.slot(n)] = choose(n, ends)
        tail.leave(tail.slot(n), 0)
    keep_partner(spec, 0)
    correlate(0)
    body.hop(0)
    keep_partner(spec, 1)
    correlate(1)
    send_parts(0, 2)
    tail.hop(0)
    body.hop(1)
    tail.hop(1)
    body.hop(2)
    tail.hop(2)
    spec = spectra([(hold[body.finals["F"]], hold_tail[tail.finals["F"]])])
    keep_partner(spec, 0)
    correlate(2)
    send_parts(2, 1)
    body.hop(3)
    tail.hop(3)
    spec = spectra([(hold[body.finals[n]], hold_tail[tail.finals[n]]) for n in "AB"])
    for k in range(2):
        keep_partner(spec, k)
        correlate(3 + k)
        send_parts(3 + k, 1)

    for copy in [*sum(first_copies, []), *near_copies, *body.copies.values(), *tail.copies.values()]:
        copy.wait_send()
    for copy in reduce_copies:
        copy.wait_recv()

    for slot in range(5):
        acc = parts[slot, t].astype(F32)
        for d in range(1, TM):
            acc = acc + inbox[d - 1, slot].astype(F32)
        sums[slot] = acc
    for copy in reduce_copies:
        copy.wait_send()


def hand_out(plan, sums, self_out, pair_out):
    p = [plan[r] for r in range(ROUNDS)]
    first = jnp.where(known(p[0]), jnp.where(known(p[1]), p[2], p[1]), p[0])

    def write(out, slot):
        for a in range(2):
            out[a, :, :LANES] = sums[slot, a * CH : (a + 1) * CH, :]
            out[a, :, LANES:] = sums[slot, 32:, a : a + 1]

    write(self_out, 0)
    for r in range(ROUNDS):
        slot = jnp.where(p[r] == 1, 1, jnp.where(p[r] == 63, 2, jnp.where(p[r] == first, 3, 4)))
        write(pair_out.at[r], slot)


def on_device(samples, fir_taps, plan):
    dft_high, dft_low = dft_tables()
    lag_mat = lag_table()
    vmem = pl.BlockSpec(memory_space=pltpu.VMEM)
    anywhere = pl.BlockSpec(memory_space=pl.ANY)
    n = len(messages(STAGES))
    dma = pltpu.SemaphoreType.DMA
    taps = fir_taps.reshape(1, -1)
    sums = pl.pallas_call(
        kernel,
        out_shape=jax.ShapeDtypeStruct((5, ROWS, LANES), F32),
        in_specs=[anywhere] * 6,
        out_specs=vmem,
        scratch_shapes=[
            pltpu.SMEM((ROUNDS,), jnp.int32),
            pltpu.VMEM(taps.shape, F32),
            pltpu.VMEM((1, 256), F32),
            pltpu.VMEM(dft_high.shape, BF16),
            pltpu.VMEM(dft_low.shape, BF16),
            pltpu.VMEM(lag_mat.shape, BF16),
            pltpu.VMEM((CH, 2048), BF16),
            pltpu.VMEM((len(NEAR), CH, 2048), BF16),
            pltpu.VMEM((n, CH, 2048), BF16),
            pltpu.VMEM((n + 3, CH, 2048), BF16),
            pltpu.VMEM((len(NEAR) + 1, CH, LANES), BF16),
            pltpu.VMEM((n, CH, LANES), BF16),
            pltpu.VMEM((n + 3, CH, LANES), BF16),
            pltpu.VMEM((256, 256), BF16),
            pltpu.VMEM((GROUPS, 32, LANES), F32),
            pltpu.VMEM((GROUPS, 32, LANES), F32),
            pltpu.VMEM((GROUPS, 32, LANES), F32),
            pltpu.VMEM((GROUPS, 32, LANES), F32),
            pltpu.VMEM((GROUPS, 32, LANES), F32),
            pltpu.VMEM((256, GROUPS * 256), BF16),
            pltpu.VMEM((5, TM, ROWS, LANES), BF16),
            pltpu.VMEM((TM - 1, 5, ROWS, LANES), BF16),
            dma((6,)),
            dma((CHUNKS, len(NEAR), 2)),
            dma((len(NEAR) + 1, 2)),
            dma((n, CHUNKS, 2)),
            dma((n, 1, 2)),
            dma((5, TM - 1, 2)),
        ],
        compiler_params=pltpu.CompilerParams(
            collective_id=0, has_side_effects=True, vmem_limit_bytes=62 * 1024 * 1024
        ),
        cost_estimate=pl.CostEstimate(flops=10**9, bytes_accessed=4 * 10**6, transcendentals=10**5),
        name="correlate_blocks",
    )(plan, samples, taps, jnp.asarray(dft_high), jnp.asarray(dft_low), jnp.asarray(lag_mat))
    return pl.pallas_call(
        hand_out,
        out_shape=(
            jax.ShapeDtypeStruct((2, CH, LAGS), F32),
            jax.ShapeDtypeStruct((ROUNDS, 2, CH, LAGS), F32),
        ),
        in_specs=[pl.BlockSpec(memory_space=pltpu.SMEM), vmem],
        out_specs=(vmem, vmem),
        cost_estimate=pl.CostEstimate(flops=0, bytes_accessed=5 * 10**5, transcendentals=0),
        name="hand_out_rounds",
    )(plan, sums)


def solution(mesh):
    in_specs = (P("chan", "tm"), P(), P())
    out_specs = (P(("chan", "tm"), None, None), P(None, ("chan", "tm"), None, None))
    return jax.shard_map(
        on_device, mesh=mesh, in_specs=in_specs, out_specs=out_specs, check_vma=False
    )
```

```python
import functools

import jax
import jax.numpy as jnp
import ml_dtypes
import numpy as np
from jax import lax
from jax.experimental import pallas as pl
from jax.experimental.pallas import tpu as pltpu
from jax.sharding import PartitionSpec as P

MESH = pl.DeviceIdType.MESH
BF16 = jnp.bfloat16
F32 = jnp.float32

CH = 16
SEG = 1024
LAGS = 129
ROUNDS = 4
TM = 8
LANES = 128
TILES = 16
CHUNKS = 4
WIDTH = 2048 // CHUNKS
ROWS = 48
GROUPS = 4
HOP_CORE, HOP_Z1, HOP_Z2, HOP_Z6, HOP_Z7, HOP_Y1, HOP_Y3 = 1, 2, 4, 12, 14, 16, 48
CHAN_HOPS = (HOP_CORE, HOP_Z1, HOP_Z1 ^ HOP_CORE, HOP_Z2, HOP_Z6, HOP_Z7, HOP_Y1, HOP_Y3)
STAGES = (
    (("A", HOP_Z2), ("B", HOP_Y3), ("F", HOP_Z7)),
    (("A", HOP_Z6), ("B", HOP_Y1), ("F", HOP_Y3)),
    (("A", HOP_Y1), ("B", HOP_Z6)),
    (("A", HOP_Y3), ("B", HOP_Z2)),
)
FLAGGED = (HOP_CORE, HOP_Z1, HOP_Z2, HOP_Z6, HOP_Y1, HOP_Y3)
NEAR = (HOP_CORE, HOP_Z1, HOP_Z1 ^ HOP_CORE)


def messages(stages):
    return [(stage, name, hop) for stage, hops in enumerate(stages) for name, hop in hops]


def group_frequencies():
    p = np.arange(64)
    first = np.concatenate([8 * p, 8 * p + 4])
    return [first] + [8 * np.arange(128) + q for q in (1, 2, 3)]


def split_bf16(x):
    high = x.astype(ml_dtypes.bfloat16)
    low = (x - high.astype(np.float64)).astype(ml_dtypes.bfloat16)
    return high, low


def dft_tables():
    r = np.arange(128)[:, None]
    tables = []
    for at, freqs in enumerate(group_frequencies()):
        angle = 2 * np.pi * ((r * freqs[None, :]) % SEG) / SEG
        cos, sin = np.cos(angle), np.sin(angle)
        if at == 0:
            top = np.concatenate([cos[:, :64], 0 * cos[:, 64:], -sin[:, :64], 0 * sin[:, 64:]], 1)
            top[:, 128] = (-1.0) ** np.arange(128)
            low = np.concatenate([0 * cos[:, :64], cos[:, 64:], 0 * sin[:, :64], -sin[:, 64:]], 1)
        else:
            top = np.concatenate([cos, -sin], 1)
            low = np.concatenate([sin, cos], 1)
        tables.append(np.concatenate([top, low], 0))
    return split_bf16(np.stack(tables))


def lag_table():
    lags = np.arange(LAGS) - LAGS // 2
    rows = []
    for at, freqs in enumerate(group_frequencies()):
        angle = 2 * np.pi * ((freqs[:, None] * lags[None, :]) % SEG) / SEG
        re, im = np.cos(angle) * 2 / SEG, -np.sin(angle) * 2 / SEG
        if at == 0:
            re[0] = 1 / SEG
            im[0] = (-1.0) ** np.abs(lags) / SEG
        rows += [re, im]
    table = np.zeros((GROUPS * 256, 256))
    table[:, :LAGS] = np.concatenate(rows, 0)
    table[:, LAGS] = table[:, LAGS - 1]
    return table.astype(ml_dtypes.bfloat16)


def known(mask):
    return jnp.logical_or(mask == 1, mask == 63)


class Stream:
    def __init__(self, stages, pieces, flags, held, arrived, sems, send):
        self.pieces, self.flags = pieces, flags
        self.held, self.arrived, self.sems, self.send = held, arrived, sems, send
        self.order = messages(stages)
        self.finals = {n: len(self.order) + k for k, n in enumerate("ABF")}
        self.copies = {}

    def slot(self, name, stage=-1):
        following = [k for k, (at, n, _) in enumerate(self.order) if n == name and at > stage]
        return following[0] if following else self.finals[name]

    def leave(self, at, h, source=None):
        if at < len(self.order):
            piece = self.pieces[h]
            source = self.held.at[at] if source is None else source
            copy = self.send(
                source.at[:, piece], self.arrived.at[at, :, piece], self.sems.at[at, h], self.order[at][2]
            )
            copy.start()
            self.copies[at, h] = copy

    def hop(self, stage):
        for h, piece in enumerate(self.pieces):
            for at, (when, name, hop) in enumerate(self.order):
                if when == stage:
                    self.copies[at, h].wait_recv()
                    value = self.arrived[at, :, piece]
                    if name != "F":
                        value = jnp.where(self.flags[name, hop], value, self.held[at, :, piece])
                    after = self.slot(name, stage)
                    self.held[after, :, piece] = value
                    self.leave(after, h)


def kernel(
    plan_in, samples, taps_in, dft_high_in, dft_low_in, lag_in, sums,
    plan, taps, taps_row, dft_high, dft_low, lag_mat, own, near_body, hop_body, hold,
    near_tails, hop_tail, hold_tail,
    band, xr, xi, yr, yi, yr2, cross, parts, inbox,
    load_sem, first_sem, near_sem, body_sem, tail_sem, red_sem,
):
    c = lax.axis_index("chan")
    t = lax.axis_index("tm")

    def chan_peer(hop):
        return (lax.bitwise_xor(c, jnp.int32(hop)), t)

    def tm_peer(d):
        return (c, lax.bitwise_xor(t, jnp.int32(d)))

    later, earlier = lax.rem(t + 1, TM), lax.rem(t + TM - 1, TM)

    barrier = pltpu.get_barrier_semaphore()
    greeted = [chan_peer(hop) for hop in CHAN_HOPS] + [tm_peer(d) for d in range(1, TM)]
    greeted += [(chan_peer(hop)[0], side) for hop in NEAR for side in (later, earlier)]
    for device in greeted:
        pl.semaphore_signal(barrier, inc=1, device_id=device, device_id_type=MESH)

    loads = [
        pltpu.make_async_copy(src, dst, load_sem.at[i])
        for i, (src, dst) in enumerate((
            (plan_in, plan), (taps_in, taps), (samples, own),
            (dft_high_in, dft_high), (dft_low_in, dft_low), (lag_in, lag_mat),
        ))
    ]
    pl.semaphore_wait(barrier, len(greeted))

    def remote(src, dst, sem, device):
        return pltpu.make_async_remote_copy(
            src_ref=src, dst_ref=dst, send_sem=sem.at[0], recv_sem=sem.at[1],
            device_id=device, device_id_type=MESH,
        )

    def by_hop(src, dst, sem, hop):
        return remote(src, dst, sem, chan_peer(hop))

    pieces = [slice(h * WIDTH, (h + 1) * WIDTH) for h in range(CHUNKS)]
    first_copies = [
        [by_hop(samples.at[:, piece], near_body.at[k, :, piece], first_sem.at[h, k], hop) for k, hop in enumerate(NEAR)]
        for h, piece in enumerate(pieces)
    ]
    end = samples.at[:, (TILES - 1) * LANES :]
    near_copies = [
        remote(end, near_tails.at[k], near_sem.at[k], (chan_peer(hop)[0], later))
        for k, hop in enumerate((0,) + NEAR)
    ]
    for copy in [*first_copies[0][::-1], *near_copies, *[x for row in first_copies[1:] for x in row[::-1]]]:
        copy.start()
    for load in loads:
        load.start()

    loads[0].wait()
    loads[1].wait()

    p = [plan[r] for r in range(ROUNDS)]
    mask_a = jnp.where(known(p[0]), jnp.where(known(p[1]), p[2], p[1]), p[0])
    mask_b = p[0] + p[1] + p[2] + p[3] - 64 - mask_a

    def flag(m, hop):
        bit = lambda k: (m >> k) & 1
        if hop == HOP_CORE:
            v = bit(0)
        elif hop == HOP_Z1:
            v = bit(1)
        elif hop == HOP_Z6:
            v = bit(3)
        elif hop == HOP_Z2:
            v = bit(2) ^ bit(3)
        elif hop == HOP_Y3:
            v = bit(5)
        else:
            v = bit(4) ^ bit(5)
        return v == 1

    flags = {(n, hop): flag(m, hop) for n, m in (("A", mask_a), ("B", mask_b)) for hop in FLAGGED}

    taps_row[...] = jnp.zeros_like(taps_row)
    taps_row[:, : taps.shape[1]] = taps[...]
    rolled = pltpu.roll(jnp.broadcast_to(taps_row[...], (256, 256)), 128, 1, stride=1, stride_axis=0)
    toeplitz = rolled[:, :LANES]
    high = toeplitz.astype(BF16)
    band[:, :LANES] = high
    band[:, LANES:] = (toeplitz - high.astype(F32)).astype(BF16)
    body = Stream(STAGES, pieces, flags, hold, hop_body, body_sem, by_hop)
    tail = Stream(STAGES, [slice(0, LANES)], flags, hold_tail, hop_tail, tail_sem, by_hop)

    def choose(name, values):
        core, z1 = flags[name, HOP_CORE], flags[name, HOP_Z1]
        return jnp.where(z1, jnp.where(core, values[3], values[2]), jnp.where(core, values[1], values[0]))

    def spectra(blocks):
        filtered = []
        for block, before_it in blocks:
            tiles = [block[:, j * LANES : (j + 1) * LANES] for j in range(TILES)]
            now = jnp.concatenate(tiles, 0)
            before = jnp.concatenate([before_it] + tiles[:-1], 0)
            both = jnp.dot(jnp.concatenate([before, now], 1), band[...], preferred_element_type=F32)
            filtered.append(both[:, :LANES] + both[:, LANES:])
        y = []
        for j in range(8):
            y.append(jnp.concatenate(
                [f[(s * 8 + j) * CH : (s * 8 + j + 1) * CH] for f in filtered for s in range(2)], 0))
        count = 32 * len(blocks)
        add = [y[j] + y[j + 4] for j in range(4)]
        sub = [y[j] - y[j + 4] for j in range(4)]
        root = np.float32(np.sqrt(0.5))
        e02, e13 = add[0] + add[2], add[1] + add[3]
        dm, dp = (sub[1] - sub[3]) * root, (sub[1] + sub[3]) * root
        z = (
            (e02 + e13, e02 - e13),
            (sub[0] + dm, -sub[2] - dp),
            (add[0] - add[2], add[3] - add[1]),
            (sub[0] - dm, sub[2] - dp),
        )
        re, im = [], []
        total = None
        for g in range(GROUPS):
            full = jnp.concatenate(z[g], 1)
            z_high = full.astype(BF16)
            z_low = (full - z_high.astype(F32)).astype(BF16)
            first = jnp.dot(jnp.concatenate([z_high, z_low], 0), dft_high[g], preferred_element_type=F32)
            second = jnp.dot(z_high, dft_low[g], preferred_element_type=F32)
            out = first[:count] + (first[count:] + second)
            re.append(out[:, :LANES])
            im.append(out[:, LANES:])
            energy = re[g] * re[g] + im[g] * im[g]
            total = energy if total is None else total + energy
        water = jnp.sum(total, axis=1, keepdims=True) * np.float32(0.1 / 513) + np.float32(1e-6)
        lane0 = lax.broadcasted_iota(jnp.int32, (count, LANES), 1) == 0
        result = []
        for g in range(GROUPS):
            re2, im2 = re[g] * re[g], im[g] * im[g]
            if g == 0:
                inv_re = lax.rsqrt(jnp.where(lane0, re2, re2 + im2) + water)
                inv_im = lax.rsqrt(jnp.where(lane0, im2, re2 + im2) + water)
            else:
                inv_re = inv_im = lax.rsqrt(re2 + im2 + water)
            result.append((
                (re[g] * inv_re).astype(BF16).astype(F32),
                (im[g] * inv_im).astype(BF16).astype(F32),
            ))
        return result

    def keep_partner(spec, block):
        rows = slice(block * 32, block * 32 + 32)
        lane0 = lax.broadcasted_iota(jnp.int32, (32, LANES), 1) == 0
        for g in range(GROUPS):
            re, im = spec[g][0][rows], spec[g][1][rows]
            yr[g] = re
            if g == 0:
                yi[g] = jnp.where(lane0, 0.0, im)
                yr2[g] = jnp.where(lane0, im, re)
            else:
                yi[g] = im
                yr2[g] = re

    def correlate(slot):
        def step(a, carry):
            for g in range(GROUPS):
                sum_re = sum_im = None
                for s in range(2):
                    rows = pl.ds(s * CH, CH)
                    x_re = xr[g, pl.ds(s * CH + a, 1), :]
                    x_im = xi[g, pl.ds(s * CH + a, 1), :]
                    y_im = yi[g, rows, :]
                    term_re = x_re * yr[g, rows, :] + x_im * y_im
                    term_im = x_im * yr2[g, rows, :] - x_re * y_im
                    sum_re = term_re if s == 0 else sum_re + term_re
                    sum_im = term_im if s == 0 else sum_im + term_im
                where = pl.ds(pl.multiple_of(a * CH, CH), CH)
                cross[where, g * 256 : g * 256 + LANES] = sum_re.astype(BF16)
                cross[where, g * 256 + LANES : (g + 1) * 256] = sum_im.astype(BF16)
            return carry

        lax.fori_loop(0, CH, step, 0, unroll=4)
        lagged = jnp.dot(cross[...], lag_mat[...], preferred_element_type=F32)
        parts[slot, :, :32, :] = lagged[:, :LANES].astype(BF16).reshape(TM, 32, LANES)
        last = lagged[:, LANES:].reshape(TM, 2, CH, LANES)
        lane0 = lax.broadcasted_iota(jnp.int32, (TM, CH, LANES), 2) == 0
        parts[slot, :, 32:, :] = jnp.where(lane0, last[:, 0], last[:, 1]).astype(BF16)

    reduce_copies = {slot: [] for slot in range(5)}

    def send_parts(first, count):
        for d in (6, 5, 7, 2, 4, 1, 3):
            copy = remote(
                parts.at[pl.ds(first, count), lax.bitwise_xor(t, jnp.int32(d))],
                inbox.at[d - 1, pl.ds(first, count)],
                red_sem.at[first, d - 1],
                tm_peer(d),
            )
            copy.start()
            reduce_copies[first].append(copy)

    for load in loads[2:]:
        load.wait()
    for h, piece in enumerate(pieces):
        for copy in first_copies[h]:
            copy.wait_recv()
        blocks = [own[:, piece]] + [near_body[k, :, piece] for k in range(len(NEAR))]
        for n in "AB":
            hold[body.slot(n), :, piece] = choose(n, blocks)
            body.leave(body.slot(n), h)
        body.leave(body.slot("F"), h, near_body.at[0])

    for copy in near_copies[:2]:
        copy.wait_recv()
    ends = [jnp.where(t == 0, jnp.zeros((CH, LANES), BF16), near_tails[k]) for k in range(2)]
    hold_tail[tail.slot("F")] = ends[1]
    tail.leave(tail.slot("F"), 0)
    spec = spectra([(own[...], ends[0]), (near_body[0], ends[1])])
    for g in range(GROUPS):
        xr[g], xi[g] = spec[g][0][:32], spec[g][1][:32]

    for copy in near_copies[2:]:
        copy.wait_recv()
    ends += [jnp.where(t == 0, jnp.zeros((CH, LANES), BF16), near_tails[k]) for k in (2, 3)]
    for n in "AB":
        hold_tail[tail.slot(n)] = choose(n, ends)
        tail.leave(tail.slot(n), 0)
    keep_partner(spec, 0)
    correlate(0)
    body.hop(0)
    keep_partner(spec, 1)
    correlate(1)
    send_parts(0, 2)
    tail.hop(0)
    body.hop(1)
    tail.hop(1)
    body.hop(2)
    tail.hop(2)
    spec = spectra([(hold[body.finals["F"]], hold_tail[tail.finals["F"]])])
    keep_partner(spec, 0)
    correlate(2)
    send_parts(2, 1)
    body.hop(3)
    tail.hop(3)
    spec = spectra([(hold[body.finals[n]], hold_tail[tail.finals[n]]) for n in "AB"])
    for k in range(2):
        keep_partner(spec, k)
        correlate(3 + k)
        send_parts(3 + k, 1)

    for slot in range(5):
        for copy in reduce_copies[slot]:
            copy.wait_recv()
        acc = parts[slot, t].astype(F32)
        for d in range(1, TM):
            acc = acc + inbox[d - 1, slot].astype(F32)
        sums[slot] = acc
    reduced = [copy for copies in reduce_copies.values() for copy in copies]
    for copy in [*sum(first_copies, []), *near_copies, *body.copies.values(), *tail.copies.values(), *reduced]:
        copy.wait_send()


def hand_out(plan, sums, self_out, pair_out):
    p = [plan[r] for r in range(ROUNDS)]
    first = jnp.where(known(p[0]), jnp.where(known(p[1]), p[2], p[1]), p[0])

    def write(out, slot):
        for a in range(2):
            out[a, :, :LANES] = sums[slot, a * CH : (a + 1) * CH, :]
            out[a, :, LANES:] = sums[slot, 32:, a : a + 1]

    write(self_out, 0)
    for r in range(ROUNDS):
        slot = jnp.where(p[r] == 1, 1, jnp.where(p[r] == 63, 2, jnp.where(p[r] == first, 3, 4)))
        write(pair_out.at[r], slot)


def on_device(samples, fir_taps, plan):
    dft_high, dft_low = dft_tables()
    lag_mat = lag_table()
    vmem = pl.BlockSpec(memory_space=pltpu.VMEM)
    anywhere = pl.BlockSpec(memory_space=pl.ANY)
    n = len(messages(STAGES))
    dma = pltpu.SemaphoreType.DMA
    taps = fir_taps.reshape(1, -1)
    sums = pl.pallas_call(
        kernel,
        out_shape=jax.ShapeDtypeStruct((5, ROWS, LANES), F32),
        in_specs=[anywhere] * 6,
        out_specs=vmem,
        scratch_shapes=[
            pltpu.SMEM((ROUNDS,), jnp.int32),
            pltpu.VMEM(taps.shape, F32),
            pltpu.VMEM((1, 256), F32),
            pltpu.VMEM(dft_high.shape, BF16),
            pltpu.VMEM(dft_low.shape, BF16),
            pltpu.VMEM(lag_mat.shape, BF16),
            pltpu.VMEM((CH, 2048), BF16),
            pltpu.VMEM((len(NEAR), CH, 2048), BF16),
            pltpu.VMEM((n, CH, 2048), BF16),
            pltpu.VMEM((n + 3, CH, 2048), BF16),
            pltpu.VMEM((len(NEAR) + 1, CH, LANES), BF16),
            pltpu.VMEM((n, CH, LANES), BF16),
            pltpu.VMEM((n + 3, CH, LANES), BF16),
            pltpu.VMEM((256, 256), BF16),
            pltpu.VMEM((GROUPS, 32, LANES), F32),
            pltpu.VMEM((GROUPS, 32, LANES), F32),
            pltpu.VMEM((GROUPS, 32, LANES), F32),
            pltpu.VMEM((GROUPS, 32, LANES), F32),
            pltpu.VMEM((GROUPS, 32, LANES), F32),
            pltpu.VMEM((256, GROUPS * 256), BF16),
            pltpu.VMEM((5, TM, ROWS, LANES), BF16),
            pltpu.VMEM((TM - 1, 5, ROWS, LANES), BF16),
            dma((6,)),
            dma((CHUNKS, len(NEAR), 2)),
            dma((len(NEAR) + 1, 2)),
            dma((n, CHUNKS, 2)),
            dma((n, 1, 2)),
            dma((5, TM - 1, 2)),
        ],
        compiler_params=pltpu.CompilerParams(
            collective_id=0, has_side_effects=True, vmem_limit_bytes=62 * 1024 * 1024
        ),
        cost_estimate=pl.CostEstimate(flops=10**9, bytes_accessed=4 * 10**6, transcendentals=10**5),
        name="correlate_blocks",
    )(plan, samples, taps, jnp.asarray(dft_high), jnp.asarray(dft_low), jnp.asarray(lag_mat))
    return pl.pallas_call(
        hand_out,
        out_shape=(
            jax.ShapeDtypeStruct((2, CH, LAGS), F32),
            jax.ShapeDtypeStruct((ROUNDS, 2, CH, LAGS), F32),
        ),
        in_specs=[pl.BlockSpec(memory_space=pltpu.SMEM), vmem],
        out_specs=(vmem, vmem),
        cost_estimate=pl.CostEstimate(flops=0, bytes_accessed=5 * 10**5, transcendentals=0),
        name="hand_out_rounds",
    )(plan, sums)


def solution(mesh):
    in_specs = (P("chan", "tm"), P(), P())
    out_specs = (P(("chan", "tm"), None, None), P(None, ("chan", "tm"), None, None))
    return jax.shard_map(
        on_device, mesh=mesh, in_specs=in_specs, out_specs=out_specs, check_vma=False
    )
```

```python
import functools

import jax
import jax.numpy as jnp
import ml_dtypes
import numpy as np
from jax import lax
from jax.experimental import pallas as pl
from jax.experimental.pallas import tpu as pltpu
from jax.sharding import PartitionSpec as P

MESH = pl.DeviceIdType.MESH
BF16 = jnp.bfloat16
F32 = jnp.float32

CH = 16
SEG = 1024
LAGS = 129
ROUNDS = 4
TM = 8
LANES = 128
TILES = 16
CHUNKS = 4
WIDTH = 2048 // CHUNKS
ROWS = 48
GROUPS = 4
HOP_CORE, HOP_Z1, HOP_Z2, HOP_Z6, HOP_Z7, HOP_Y1, HOP_Y3 = 1, 2, 4, 12, 14, 16, 48
CHAN_HOPS = (HOP_Z7, HOP_Z6, HOP_Y3, HOP_Y1, HOP_Z2, HOP_Z1, HOP_Z1 ^ HOP_CORE, HOP_CORE)
STAGES = (
    (("A", HOP_Z2), ("B", HOP_Y3), ("F", HOP_Z7)),
    (("A", HOP_Z6), ("B", HOP_Y1), ("F", HOP_Y3)),
    (("A", HOP_Y1), ("B", HOP_Z6)),
    (("A", HOP_Y3), ("B", HOP_Z2)),
)
FLAGGED = (HOP_CORE, HOP_Z1, HOP_Z2, HOP_Z6, HOP_Y1, HOP_Y3)
NEAR = (HOP_CORE, HOP_Z1, HOP_Z1 ^ HOP_CORE)


def messages(stages):
    return [(stage, name, hop) for stage, hops in enumerate(stages) for name, hop in hops]


def group_frequencies():
    p = np.arange(64)
    first = np.concatenate([8 * p, 8 * p + 4])
    return [first] + [8 * np.arange(128) + q for q in (1, 2, 3)]


def split_bf16(x):
    high = x.astype(ml_dtypes.bfloat16)
    low = (x - high.astype(np.float64)).astype(ml_dtypes.bfloat16)
    return high, low


def dft_tables():
    r = np.arange(128)[:, None]
    tables = []
    for at, freqs in enumerate(group_frequencies()):
        angle = 2 * np.pi * ((r * freqs[None, :]) % SEG) / SEG
        cos, sin = np.cos(angle), np.sin(angle)
        if at == 0:
            top = np.concatenate([cos[:, :64], 0 * cos[:, 64:], -sin[:, :64], 0 * sin[:, 64:]], 1)
            top[:, 128] = (-1.0) ** np.arange(128)
            low = np.concatenate([0 * cos[:, :64], cos[:, 64:], 0 * sin[:, :64], -sin[:, 64:]], 1)
        else:
            top = np.concatenate([cos, -sin], 1)
            low = np.concatenate([sin, cos], 1)
        tables.append(np.concatenate([top, low], 0))
    return split_bf16(np.stack(tables))


def lag_table():
    lags = np.arange(LAGS) - LAGS // 2
    rows = []
    for at, freqs in enumerate(group_frequencies()):
        angle = 2 * np.pi * ((freqs[:, None] * lags[None, :]) % SEG) / SEG
        re, im = np.cos(angle) * 2 / SEG, -np.sin(angle) * 2 / SEG
        if at == 0:
            re[0] = 1 / SEG
            im[0] = (-1.0) ** np.abs(lags) / SEG
        rows += [re, im]
    table = np.zeros((GROUPS * 256, 256))
    table[:, :LAGS] = np.concatenate(rows, 0)
    table[:, LAGS] = table[:, LAGS - 1]
    return table.astype(ml_dtypes.bfloat16)


def known(mask):
    return jnp.logical_or(mask == 1, mask == 63)


class Stream:
    def __init__(self, stages, pieces, flags, held, arrived, sems, send):
        self.pieces, self.flags = pieces, flags
        self.held, self.arrived, self.sems, self.send = held, arrived, sems, send
        self.order = messages(stages)
        self.finals = {n: len(self.order) + k for k, n in enumerate("ABF")}
        self.copies = {}

    def slot(self, name, stage=-1):
        following = [k for k, (at, n, _) in enumerate(self.order) if n == name and at > stage]
        return following[0] if following else self.finals[name]

    def leave(self, at, h, source=None):
        if at < len(self.order):
            piece = self.pieces[h]
            source = self.held.at[at] if source is None else source
            copy = self.send(
                source.at[:, piece], self.arrived.at[at, :, piece], self.sems.at[at, h], self.order[at][2]
            )
            copy.start()
            self.copies[at, h] = copy

    def hop(self, stage):
        for h, piece in enumerate(self.pieces):
            for at, (when, name, hop) in enumerate(self.order):
                if when == stage:
                    self.copies[at, h].wait_recv()
                    value = self.arrived[at, :, piece]
                    if name != "F":
                        value = jnp.where(self.flags[name, hop], value, self.held[at, :, piece])
                    after = self.slot(name, stage)
                    self.held[after, :, piece] = value
                    self.leave(after, h)


def kernel(
    plan_in, samples, taps_in, dft_high_in, dft_low_in, lag_in, sums,
    plan, taps, taps_row, dft_high, dft_low, lag_mat, own, near_body, hop_body, hold,
    near_tails, hop_tail, hold_tail,
    band, xr, xi, yr, yi, yr2, cross, parts, inbox,
    load_sem, first_sem, near_sem, body_sem, tail_sem, red_sem,
):
    c = lax.axis_index("chan")
    t = lax.axis_index("tm")

    def chan_peer(hop):
        return (lax.bitwise_xor(c, jnp.int32(hop)), t)

    def tm_peer(d):
        return (c, lax.bitwise_xor(t, jnp.int32(d)))

    later, earlier = lax.rem(t + 1, TM), lax.rem(t + TM - 1, TM)

    barrier = pltpu.get_barrier_semaphore()
    greeted = [chan_peer(hop) for hop in CHAN_HOPS] + [tm_peer(d) for d in range(1, TM)]
    greeted += [(chan_peer(hop)[0], side) for hop in NEAR for side in (later, earlier)]
    for device in greeted:
        pl.semaphore_signal(barrier, inc=1, device_id=device, device_id_type=MESH)

    loads = [
        pltpu.make_async_copy(src, dst, load_sem.at[i])
        for i, (src, dst) in enumerate((
            (plan_in, plan), (taps_in, taps), (samples, own),
            (dft_high_in, dft_high), (dft_low_in, dft_low), (lag_in, lag_mat),
        ))
    ]
    pl.semaphore_wait(barrier, len(greeted))

    def remote(src, dst, sem, device):
        return pltpu.make_async_remote_copy(
            src_ref=src, dst_ref=dst, send_sem=sem.at[0], recv_sem=sem.at[1],
            device_id=device, device_id_type=MESH,
        )

    def by_hop(src, dst, sem, hop):
        return remote(src, dst, sem, chan_peer(hop))

    pieces = [slice(h * WIDTH, (h + 1) * WIDTH) for h in range(CHUNKS)]
    first_copies = [
        [by_hop(samples.at[:, piece], near_body.at[k, :, piece], first_sem.at[h, k], hop) for k, hop in enumerate(NEAR)]
        for h, piece in enumerate(pieces)
    ]
    end = samples.at[:, (TILES - 1) * LANES :]
    near_copies = [
        remote(end, near_tails.at[k], near_sem.at[k], (chan_peer(hop)[0], later))
        for k, hop in enumerate((0,) + NEAR)
    ]
    for copy in [*first_copies[0][::-1], *near_copies, *[x for row in first_copies[1:] for x in row[::-1]]]:
        copy.start()
    for load in loads:
        load.start()

    loads[0].wait()
    loads[1].wait()

    p = [plan[r] for r in range(ROUNDS)]
    mask_a = jnp.where(known(p[0]), jnp.where(known(p[1]), p[2], p[1]), p[0])
    mask_b = p[0] + p[1] + p[2] + p[3] - 64 - mask_a

    def flag(m, hop):
        bit = lambda k: (m >> k) & 1
        if hop == HOP_CORE:
            v = bit(0)
        elif hop == HOP_Z1:
            v = bit(1)
        elif hop == HOP_Z6:
            v = bit(3)
        elif hop == HOP_Z2:
            v = bit(2) ^ bit(3)
        elif hop == HOP_Y3:
            v = bit(5)
        else:
            v = bit(4) ^ bit(5)
        return v == 1

    flags = {(n, hop): flag(m, hop) for n, m in (("A", mask_a), ("B", mask_b)) for hop in FLAGGED}

    taps_row[...] = jnp.zeros_like(taps_row)
    taps_row[:, : taps.shape[1]] = taps[...]
    rolled = pltpu.roll(jnp.broadcast_to(taps_row[...], (256, 256)), 128, 1, stride=1, stride_axis=0)
    toeplitz = rolled[:, :LANES]
    high = toeplitz.astype(BF16)
    band[:, :LANES] = high
    band[:, LANES:] = (toeplitz - high.astype(F32)).astype(BF16)
    body = Stream(STAGES, pieces, flags, hold, hop_body, body_sem, by_hop)
    tail = Stream(STAGES, [slice(0, LANES)], flags, hold_tail, hop_tail, tail_sem, by_hop)

    def choose(name, values):
        core, z1 = flags[name, HOP_CORE], flags[name, HOP_Z1]
        return jnp.where(z1, jnp.where(core, values[3], values[2]), jnp.where(core, values[1], values[0]))

    def spectra(blocks):
        filtered = []
        for block, before_it in blocks:
            tiles = [block[:, j * LANES : (j + 1) * LANES] for j in range(TILES)]
            now = jnp.concatenate(tiles, 0)
            before = jnp.concatenate([before_it] + tiles[:-1], 0)
            both = jnp.dot(jnp.concatenate([before, now], 1), band[...], preferred_element_type=F32)
            filtered.append(both[:, :LANES] + both[:, LANES:])
        y = []
        for j in range(8):
            y.append(jnp.concatenate(
                [f[(s * 8 + j) * CH : (s * 8 + j + 1) * CH] for f in filtered for s in range(2)], 0))
        count = 32 * len(blocks)
        add = [y[j] + y[j + 4] for j in range(4)]
        sub = [y[j] - y[j + 4] for j in range(4)]
        root = np.float32(np.sqrt(0.5))
        e02, e13 = add[0] + add[2], add[1] + add[3]
        dm, dp = (sub[1] - sub[3]) * root, (sub[1] + sub[3]) * root
        z = (
            (e02 + e13, e02 - e13),
            (sub[0] + dm, -sub[2] - dp),
            (add[0] - add[2], add[3] - add[1]),
            (sub[0] - dm, sub[2] - dp),
        )
        re, im = [], []
        total = None
        for g in range(GROUPS):
            full = jnp.concatenate(z[g], 1)
            z_high = full.astype(BF16)
            z_low = (full - z_high.astype(F32)).astype(BF16)
            first = jnp.dot(jnp.concatenate([z_high, z_low], 0), dft_high[g], preferred_element_type=F32)
            second = jnp.dot(z_high, dft_low[g], preferred_element_type=F32)
            out = first[:count] + (first[count:] + second)
            re.append(out[:, :LANES])
            im.append(out[:, LANES:])
            energy = re[g] * re[g] + im[g] * im[g]
            total = energy if total is None else total + energy
        water = jnp.sum(total, axis=1, keepdims=True) * np.float32(0.1 / 513) + np.float32(1e-6)
        lane0 = lax.broadcasted_iota(jnp.int32, (count, LANES), 1) == 0
        result = []
        for g in range(GROUPS):
            re2, im2 = re[g] * re[g], im[g] * im[g]
            if g == 0:
                inv_re = lax.rsqrt(jnp.where(lane0, re2, re2 + im2) + water)
                inv_im = lax.rsqrt(jnp.where(lane0, im2, re2 + im2) + water)
            else:
                inv_re = inv_im = lax.rsqrt(re2 + im2 + water)
            result.append((
                (re[g] * inv_re).astype(BF16).astype(F32),
                (im[g] * inv_im).astype(BF16).astype(F32),
            ))
        return result

    def keep_partner(spec, block):
        rows = slice(block * 32, block * 32 + 32)
        lane0 = lax.broadcasted_iota(jnp.int32, (32, LANES), 1) == 0
        for g in range(GROUPS):
            re, im = spec[g][0][rows], spec[g][1][rows]
            yr[g] = re
            if g == 0:
                yi[g] = jnp.where(lane0, 0.0, im)
                yr2[g] = jnp.where(lane0, im, re)
            else:
                yi[g] = im
                yr2[g] = re

    def correlate(slot):
        def step(a, carry):
            for g in range(GROUPS):
                sum_re = sum_im = None
                for s in range(2):
                    rows = pl.ds(s * CH, CH)
                    x_re = xr[g, pl.ds(s * CH + a, 1), :]
                    x_im = xi[g, pl.ds(s * CH + a, 1), :]
                    y_im = yi[g, rows, :]
                    term_re = x_re * yr[g, rows, :] + x_im * y_im
                    term_im = x_im * yr2[g, rows, :] - x_re * y_im
                    sum_re = term_re if s == 0 else sum_re + term_re
                    sum_im = term_im if s == 0 else sum_im + term_im
                where = pl.ds(pl.multiple_of(a * CH, CH), CH)
                cross[where, g * 256 : g * 256 + LANES] = sum_re.astype(BF16)
                cross[where, g * 256 + LANES : (g + 1) * 256] = sum_im.astype(BF16)
            return carry

        lax.fori_loop(0, CH, step, 0, unroll=4)
        lagged = jnp.dot(cross[...], lag_mat[...], preferred_element_type=F32)
        parts[slot, :, :32, :] = lagged[:, :LANES].astype(BF16).reshape(TM, 32, LANES)
        last = lagged[:, LANES:].reshape(TM, 2, CH, LANES)
        lane0 = lax.broadcasted_iota(jnp.int32, (TM, CH, LANES), 2) == 0
        parts[slot, :, 32:, :] = jnp.where(lane0, last[:, 0], last[:, 1]).astype(BF16)

    reduce_copies = {slot: [] for slot in range(5)}

    def send_parts(first, count):
        for d in (6, 5, 7, 2, 4, 1, 3):
            copy = remote(
                parts.at[pl.ds(first, count), lax.bitwise_xor(t, jnp.int32(d))],
                inbox.at[d - 1, pl.ds(first, count)],
                red_sem.at[first, d - 1],
                tm_peer(d),
            )
            copy.start()
            reduce_copies[first].append(copy)

    for load in loads[2:]:
        load.wait()
    for h, piece in enumerate(pieces):
        for copy in first_copies[h]:
            copy.wait_recv()
        blocks = [own[:, piece]] + [near_body[k, :, piece] for k in range(len(NEAR))]
        for n in "AB":
            hold[body.slot(n), :, piece] = choose(n, blocks)
            body.leave(body.slot(n), h)
        body.leave(body.slot("F"), h, near_body.at[0])

    for copy in near_copies[:2]:
        copy.wait_recv()
    ends = [jnp.where(t == 0, jnp.zeros((CH, LANES), BF16), near_tails[k]) for k in range(2)]
    hold_tail[tail.slot("F")] = ends[1]
    tail.leave(tail.slot("F"), 0)
    spec = spectra([(own[...], ends[0]), (near_body[0], ends[1])])
    for g in range(GROUPS):
        xr[g], xi[g] = spec[g][0][:32], spec[g][1][:32]

    for copy in near_copies[2:]:
        copy.wait_recv()
    ends += [jnp.where(t == 0, jnp.zeros((CH, LANES), BF16), near_tails[k]) for k in (2, 3)]
    for n in "AB":
        hold_tail[tail.slot(n)] = choose(n, ends)
        tail.leave(tail.slot(n), 0)
    keep_partner(spec, 0)
    correlate(0)
    body.hop(0)
    keep_partner(spec, 1)
    correlate(1)
    send_parts(0, 2)
    tail.hop(0)
    body.hop(1)
    tail.hop(1)
    body.hop(2)
    tail.hop(2)
    spec = spectra([(hold[body.finals["F"]], hold_tail[tail.finals["F"]])])
    keep_partner(spec, 0)
    correlate(2)
    send_parts(2, 1)
    body.hop(3)
    tail.hop(3)
    spec = spectra([(hold[body.finals[n]], hold_tail[tail.finals[n]]) for n in "AB"])
    for k in range(2):
        keep_partner(spec, k)
        correlate(3 + k)
        send_parts(3 + k, 1)

    for slot in range(5):
        for copy in reduce_copies[slot]:
            copy.wait_recv()
        acc = parts[slot, t].astype(F32)
        for d in range(1, TM):
            acc = acc + inbox[d - 1, slot].astype(F32)
        sums[slot] = acc
    reduced = [copy for copies in reduce_copies.values() for copy in copies]
    for copy in [*sum(first_copies, []), *near_copies, *body.copies.values(), *tail.copies.values(), *reduced]:
        copy.wait_send()


def hand_out(plan, sums, self_out, pair_out):
    p = [plan[r] for r in range(ROUNDS)]
    first = jnp.where(known(p[0]), jnp.where(known(p[1]), p[2], p[1]), p[0])

    def write(out, slot):
        for a in range(2):
            out[a, :, :LANES] = sums[slot, a * CH : (a + 1) * CH, :]
            out[a, :, LANES:] = sums[slot, 32:, a : a + 1]

    write(self_out, 0)
    for r in range(ROUNDS):
        slot = jnp.where(p[r] == 1, 1, jnp.where(p[r] == 63, 2, jnp.where(p[r] == first, 3, 4)))
        write(pair_out.at[r], slot)


def on_device(samples, fir_taps, plan):
    dft_high, dft_low = dft_tables()
    lag_mat = lag_table()
    vmem = pl.BlockSpec(memory_space=pltpu.VMEM)
    anywhere = pl.BlockSpec(memory_space=pl.ANY)
    n = len(messages(STAGES))
    dma = pltpu.SemaphoreType.DMA
    taps = fir_taps.reshape(1, -1)
    sums = pl.pallas_call(
        kernel,
        out_shape=jax.ShapeDtypeStruct((5, ROWS, LANES), F32),
        in_specs=[anywhere] * 6,
        out_specs=vmem,
        scratch_shapes=[
            pltpu.SMEM((ROUNDS,), jnp.int32),
            pltpu.VMEM(taps.shape, F32),
            pltpu.VMEM((1, 256), F32),
            pltpu.VMEM(dft_high.shape, BF16),
            pltpu.VMEM(dft_low.shape, BF16),
            pltpu.VMEM(lag_mat.shape, BF16),
            pltpu.VMEM((CH, 2048), BF16),
            pltpu.VMEM((len(NEAR), CH, 2048), BF16),
            pltpu.VMEM((n, CH, 2048), BF16),
            pltpu.VMEM((n + 3, CH, 2048), BF16),
            pltpu.VMEM((len(NEAR) + 1, CH, LANES), BF16),
            pltpu.VMEM((n, CH, LANES), BF16),
            pltpu.VMEM((n + 3, CH, LANES), BF16),
            pltpu.VMEM((256, 256), BF16),
            pltpu.VMEM((GROUPS, 32, LANES), F32),
            pltpu.VMEM((GROUPS, 32, LANES), F32),
            pltpu.VMEM((GROUPS, 32, LANES), F32),
            pltpu.VMEM((GROUPS, 32, LANES), F32),
            pltpu.VMEM((GROUPS, 32, LANES), F32),
            pltpu.VMEM((256, GROUPS * 256), BF16),
            pltpu.VMEM((5, TM, ROWS, LANES), BF16),
            pltpu.VMEM((TM - 1, 5, ROWS, LANES), BF16),
            dma((6,)),
            dma((CHUNKS, len(NEAR), 2)),
            dma((len(NEAR) + 1, 2)),
            dma((n, CHUNKS, 2)),
            dma((n, 1, 2)),
            dma((5, TM - 1, 2)),
        ],
        compiler_params=pltpu.CompilerParams(
            collective_id=0, has_side_effects=True, vmem_limit_bytes=62 * 1024 * 1024
        ),
        cost_estimate=pl.CostEstimate(flops=10**9, bytes_accessed=4 * 10**6, transcendentals=10**5),
        name="correlate_blocks",
    )(plan, samples, taps, jnp.asarray(dft_high), jnp.asarray(dft_low), jnp.asarray(lag_mat))
    return pl.pallas_call(
        hand_out,
        out_shape=(
            jax.ShapeDtypeStruct((2, CH, LAGS), F32),
            jax.ShapeDtypeStruct((ROUNDS, 2, CH, LAGS), F32),
        ),
        in_specs=[pl.BlockSpec(memory_space=pltpu.SMEM), vmem],
        out_specs=(vmem, vmem),
        cost_estimate=pl.CostEstimate(flops=0, bytes_accessed=5 * 10**5, transcendentals=0),
        name="hand_out_rounds",
    )(plan, sums)


def solution(mesh):
    in_specs = (P("chan", "tm"), P(), P())
    out_specs = (P(("chan", "tm"), None, None), P(None, ("chan", "tm"), None, None))
    return jax.shard_map(
        on_device, mesh=mesh, in_specs=in_specs, out_specs=out_specs, check_vma=False
    )
```
